256 devices in a mesh: pool: 32 (over y, x, core), prompt: 8 (over z).
Axes of the slice: x: 4, y: 4, z: 8, core: 2. Of those that a mesh axis runs over, the one named last changes fastest.
Arguments:
- prompts: bfloat16 [8192, 512], P('prompt'), may hold values from -256 to 256
- cands: bfloat16 [65536, 512], P('pool'), may hold values from -24 to 24
- positive: int32 [8192, 65536], P('prompt', 'pool'), may hold values from 0 to 1, as said below
- cot: float32 [8192], P('prompt'), may hold values from -256 to 256
Outputs:
- grad_prompts: bfloat16 [8192, 512], P('prompt')
- grad_cands: bfloat16 [65536, 512], P(('pool', 'prompt'))
The draws below stay inside these ranges and needn't reach their ends.
Inputs may be any that keep to these rules, and one draw needn't show every extreme that they name: `positive`: every row holds at least two ones; the ones of a row are not confined to one block of 2048 candidates.
All inputs are finite; a program needn't handle non-finite values.
Results may differ from the reference program's by a relative error of at most 0.02.
Values may be sent and summed in bfloat16 or wider, within the bound.
A program may use at most 64 MiB of HBM per device.

```python
import math
import jax
import jax.numpy as jnp
from jax import lax

D = 512
P_DEV = 1024
PROMPTS = 8192
CANDS = 65536
N_PROMPT = 8


def partners(key):
    pick_key = jax.random.fold_in(key, 7)
    first, second = jax.random.split(pick_key)
    partner = 2 * jax.random.randint(first, (PROMPTS,), 0, CANDS // 2)
    aligned = jax.random.randint(second, (PROMPTS,), 0, 32) == 0
    return (partner, aligned)


def pool_view(key, spread):
    partner, aligned = partners(key)
    inner_key = jax.random.fold_in(key, 41)
    first, second = jax.random.split(inner_key)
    gauss = jax.random.normal(first, (CANDS, D), jnp.float32)
    growth = 1.0 + 0.24 * jnp.arange(CANDS, dtype=jnp.float32)[:, None] / CANDS
    scales = jnp.exp(spread * jax.random.uniform(second, (CANDS, 1), jnp.float32, -1.0, 1.0)) * growth
    pool_rows = gauss * scales
    target = jnp.where(aligned, partner + 1, CANDS)
    blended = pool_rows[partner + 1]
    pool_rows = pool_rows.at[target].set(blended, mode='drop')
    return pool_rows


def draw_cands(key, part):
    pool_rows = pool_view(key, 0.22)
    return pool_rows.astype(jnp.bfloat16)


def draw_prompts(key, part):
    local_key = jax.random.fold_in(key, 53)
    first = jax.random.fold_in(local_key, 0)
    queries = jax.random.normal(first, (PROMPTS, D), jnp.float32)
    return queries.astype(jnp.bfloat16)


def draw_positive(key, part):
    partner, aligned = partners(key)
    local_key = jax.random.fold_in(key, 67)
    marked = jax.random.randint(local_key, (PROMPTS, CANDS), 0, 1024) == 0
    row_ids = jnp.arange(PROMPTS)
    marked = marked.at[row_ids, partner].set(True).at[row_ids, partner + 1].set(True)
    return marked.astype(jnp.int32)


def levels(rng, dims, shards, least, high):
    level = 1.0
    for position, parts in shards:
        heights = jax.random.uniform(jax.random.fold_in(jax.random.fold_in(rng, 6), position), (parts,), jnp.float32, least / len(shards), high / len(shards))
        level = level * jnp.repeat(jnp.exp(heights), dims[position] // parts).reshape((-1,) + (1,) * (len(dims) - 1 - position))
    return level


def centred(stream_key, dims, deviation, bound, cuts=(), held_as=jnp.bfloat16):
    loudness = levels(stream_key, dims, cuts, -0.22, 0.18) if cuts else 1.0
    values = jax.random.normal(stream_key, dims, jnp.float32) * deviation * loudness
    return jnp.minimum(jnp.maximum(values, -bound), bound).astype(held_as)


def setup_inputs(seed: int = 0) -> dict:
    splits = jax.random.split(jax.random.key(seed), 5)
    return {
        "prompts": draw_prompts(jax.random.fold_in(splits[4], 71), 0),
        "cands": draw_cands(jax.random.fold_in(splits[4], 71), 0),
        "positive": draw_positive(jax.random.fold_in(splits[4], 71), 0),
        "cot": centred(splits[3], (PROMPTS,), 40.0, 256.0, ((0, 8),), jnp.float32),
    }


NEG_FLOOR = -1e+30

def block_grads(query_block, cot_block, mask_block, cands):
    factor = 2.0 / math.sqrt(D)
    scores = jnp.dot(query_block, cands.T, preferred_element_type=jnp.float32) * factor
    chosen = mask_block == 1
    top_all = lax.optimization_barrier(jnp.max(scores, axis=1, keepdims=True))
    sum_all = lax.optimization_barrier(jnp.sum(jnp.exp(scores - top_all), axis=1, keepdims=True))
    top_pos = lax.optimization_barrier(jnp.max(jnp.where(chosen, scores, NEG_FLOOR), axis=1, keepdims=True))
    sum_pos = lax.optimization_barrier(jnp.sum(jnp.where(chosen, jnp.exp(scores - top_pos), 0.0), axis=1, keepdims=True))
    contrast = jnp.exp(scores - top_all) / sum_all - jnp.where(chosen, jnp.exp(scores - top_pos) / sum_pos, 0.0)
    weights = (cot_block[:, None] * (contrast * factor)).astype(jnp.bfloat16)
    grad_rows = jnp.dot(weights, cands, preferred_element_type=jnp.float32)
    block_part = lax.dot_general(weights, query_block, (((0,), (0,)), ((), ())), preferred_element_type=jnp.float32)
    return (grad_rows, block_part.astype(jnp.bfloat16))

def reference(prompts, cands, positive, cot):
    query_blocks = prompts.reshape(N_PROMPT, P_DEV, D)
    mask_blocks = positive.reshape(N_PROMPT, P_DEV, CANDS)
    cot_blocks = cot.reshape(N_PROMPT, P_DEV)

    def advance(running, items):
        query_block, cot_block, mask_block = items
        grad_rows, block_part = block_grads(query_block, cot_block, mask_block, cands)
        widened = lax.optimization_barrier(block_part).astype(jnp.float32)
        return (running + widened, grad_rows)
    running, grad_rows = lax.scan(advance, jnp.zeros((CANDS, D), jnp.float32), (query_blocks, cot_blocks, mask_blocks))
    grad_prompts = grad_rows.reshape(PROMPTS, D).astype(jnp.bfloat16)
    return (grad_prompts, running.astype(jnp.bfloat16))
```

```python
import functools
import math

import jax
import jax.numpy as jnp
from jax import lax
from jax.experimental import pallas as pl
from jax.experimental.pallas import tpu as pltpu
from jax.sharding import PartitionSpec as P

NEG_FLOOR = -1e30
LOG2E = 1.4426950408889634
F32 = jnp.float32
BF16 = jnp.bfloat16
SIDE = 4
MESH = pl.DeviceIdType.MESH

LONG = ((1, 4), (0, 3), (1, 3), (0, 2), (1, 2), (0, 1), (1, 1))


def kernel(
    nz,
    prompts_hbm,
    cands_hbm,
    positive_hbm,
    cot_ref,
    gp_ref,
    gc_ref,
    prompts,
    cands,
    pos,
    scores,
    pos_t,
    signed,
    weights,
    own,
    st_send,
    st_recv,
    z_send,
    z_recv,
    p1_send,
    p1_recv,
    p_acc,
    p2_send,
    p2_recv,
    p3_send,
    p3_recv,
    load_sem,
    st_sems,
    z_sems,
    p_sems,
):
    rows, width = prompts.shape
    pool = cands.shape[0]
    factor = 2.0 / math.sqrt(width)
    rate = factor * LOG2E
    block = 256
    nblocks = rows // block
    chunk = pool // nz
    half = chunk // 2

    me = lax.axis_index("pool")
    z = lax.axis_index("prompt")
    core = lax.rem(me, 2)
    x = lax.rem(me // 2, SIDE)
    y = me // (2 * SIDE)
    first = (1 - core) * x + core * y
    second = core * x + (1 - core) * y

    def place(a, b):
        return (((core * a + (1 - core) * b) * SIDE) + (1 - core) * a + core * b) * 2 + core

    sibling = {"pool": me + 1 - 2 * core}
    firsts = [{"pool": place(lax.rem(first + k, SIDE), second)} for k in range(1, SIDE)]
    seconds = [{"pool": place(first, lax.rem(second + k, SIDE))} for k in range(1, SIDE)]
    above = {"prompt": lax.rem(z + 1, nz)}
    below = {"prompt": lax.rem(z + nz - 1, nz)}

    loads = [
        pltpu.make_async_copy(cands_hbm, cands, load_sem.at[0]),
        pltpu.make_async_copy(prompts_hbm, prompts, load_sem.at[1]),
    ] + [
        pltpu.make_async_copy(
            positive_hbm.at[pl.ds(b * block, block), :], pos.at[b], load_sem.at[2 + b]
        )
        for b in range(nblocks)
    ]
    for load in loads:
        load.start()

    barrier = pltpu.get_barrier_semaphore()
    peers = [sibling] + firsts + seconds + [above, below]
    for peer in peers:
        pl.semaphore_signal(barrier, inc=1, device_id=peer, device_id_type=MESH)

    def remote(src, dst, sems, peer):
        return pltpu.make_async_remote_copy(
            src_ref=src,
            dst_ref=dst,
            send_sem=sems.at[0],
            recv_sem=sems.at[1],
            device_id=peer,
            device_id_type=MESH,
        )

    loads[0].wait()
    loads[1].wait()
    for b in range(nblocks):
        loads[2 + b].wait()
        cols = pl.ds(b * block, block)
        queries = prompts[cols, :]

        def tops(j, carry):
            top_all, top_pos = carry
            at = pl.ds(pl.multiple_of(j * block, block), block)
            s = lax.dot_general(
                cands[at, :], queries, (((1,), (1,)), ((), ())), preferred_element_type=F32
            )
            mark = pos[b, :, at].T
            scores[at, :] = s
            pos_t[at, :] = mark
            sp = jnp.where(mark == 1, s, NEG_FLOOR)
            top_all = jnp.maximum(top_all, jnp.max(s.reshape(block // 8, 8, block), axis=0))
            top_pos = jnp.maximum(top_pos, jnp.max(sp.reshape(block // 8, 8, block), axis=0))
            return top_all, top_pos

        floor = jnp.full((8, block), NEG_FLOOR, F32)
        top_all, top_pos = lax.fori_loop(0, pool // block, tops, (floor, floor), unroll=2)
        top_all = jnp.max(top_all, axis=0, keepdims=True)
        top_pos = jnp.max(top_pos, axis=0, keepdims=True)

        def sums(j, carry):
            sum_rest, sum_pos = carry
            at = pl.ds(pl.multiple_of(j * block, block), block)
            chosen = pos_t[at, :] == 1
            e = jnp.exp2((scores[at, :] - jnp.where(chosen, top_pos, top_all)) * rate)
            rest = jnp.where(chosen, 0.0, e)
            picked = e - rest
            signed[at, cols] = (rest - picked).astype(BF16)
            sum_rest = sum_rest + jnp.sum(rest.reshape(block // 8, 8, block), axis=0)
            sum_pos = sum_pos + jnp.sum(picked.reshape(block // 8, 8, block), axis=0)
            return sum_rest, sum_pos

        zero = jnp.zeros((8, block), F32)
        sum_rest, sum_pos = lax.fori_loop(0, pool // block, sums, (zero, zero), unroll=2)
        sum_rest = jnp.sum(sum_rest, axis=0, keepdims=True)
        sum_pos = jnp.sum(sum_pos, axis=0, keepdims=True)
        sum_all = sum_rest + sum_pos * jnp.exp2((top_pos - top_all) * rate)
        st_send[0, 0:1, cols] = top_all
        st_send[0, 1:2, cols] = top_pos
        st_send[0, 2:3, cols] = sum_all
        st_send[0, 3:4, cols] = sum_pos

    pl.semaphore_wait(barrier, len(peers))

    def merge(parts):
        tops = [t[0:2, :] for t in parts]
        top = functools.reduce(jnp.maximum, tops)
        total = sum(t[2:4, :] * jnp.exp2((t[0:2, :] - top) * rate) for t in parts)
        return top, total

    swap = remote(st_send.at[0], st_recv.at[0], st_sems.at[0], sibling)
    swap.start()
    swap.wait()
    top, total = merge([st_send.at[0], st_recv.at[0]])
    for stage, group in ((1, firsts), (2, seconds)):
        st_send[stage, 0:2, :] = top
        st_send[stage, 2:4, :] = total
        at = 1 + (stage - 1) * (SIDE - 1)
        copies = [
            remote(st_send.at[stage], st_recv.at[at + k], st_sems.at[at + k], peer)
            for k, peer in enumerate(group)
        ]
        for copy in copies:
            copy.start()
        for copy in copies:
            copy.wait()
        top, total = merge([st_send.at[stage]] + [st_recv.at[at + k] for k in range(SIDE - 1)])

    local_top = st_send[0, 0:2, :]
    gain = cot_ref[...] * factor
    down = gain * jnp.exp2((local_top - top) * rate) / total
    cross = gain * jnp.exp2((local_top[1:2, :] - top[0:1, :]) * rate) / total[0:1, :]
    scale_rest = down[0:1, :]
    scale_pos = down[1:2, :] - cross

    def weigh(d):
        at = pl.ds(pl.multiple_of(d * chunk, chunk), chunk)
        e = signed[at, :].astype(F32)
        weights[at, :] = (e * jnp.where(e < 0.0, scale_pos, scale_rest)).astype(BF16)

    def project(d):
        at = pl.ds(pl.multiple_of(d * chunk, chunk), chunk)
        own[d] = jnp.dot(weights[at, :], prompts[...], preferred_element_type=F32)

    def target(way, hops):
        return lax.rem(z + way * hops + nz, nz)

    def piece(way, i):
        h, hops = LONG[i]
        return (h if way == 0 else 1 - h), hops

    def z_copy(way, i):
        return remote(
            z_send.at[way, i], z_recv.at[way, i], z_sems.at[way, i], above if way == 0 else below
        )

    def z_push(way, i):
        h, hops = piece(way, i)
        d = target(1 - 2 * way, hops)
        value = own[d, h * half : (h + 1) * half, :]
        if i >= 2:
            z_copy(way, i - 2).wait_recv()
            value = value + z_recv[way, i - 2].astype(F32)
        z_send[way, i] = value.astype(BF16)
        z_copy(way, i).start()

    far = target(1, nz // 2)
    weigh(far)
    project(far)
    z_push(0, 0)
    z_push(1, 0)
    for way in (0, 1):
        d = target(1 - 2 * way, 3)
        weigh(d)
        project(d)
        z_push(way, 1)

    for hops in (2, 1, 0):
        for way in (0, 1) if hops else (0,):
            weigh(target(1 - 2 * way, hops))

    quarter = rows // 2 // SIDE
    slice_rows = quarter // SIDE
    mine = core * (rows // 2)

    def gather_rows(start, size):
        at = pl.ds(pl.multiple_of(start, block), size)
        return lax.dot_general(
            weights[:, at], cands[...], (((0,), (0,)), ((), ())), preferred_element_type=F32
        )

    for b in range(rows // 2 // block):
        at = pl.ds(b * block, block)
        p1_send[at, :] = gather_rows((rows // 2) - mine + b * block, block).astype(BF16)
    p1 = remote(p1_send, p1_recv, p_sems.at[0], sibling)
    p1.start()
    for b in range(rows // 2 // block):
        at = pl.ds(b * block, block)
        p_acc[at, :] = gather_rows(mine + b * block, block)

    z_push(0, 2)
    z_push(1, 2)

    p1.wait()
    p_acc[...] += p1_recv[...].astype(F32)
    p2_send[...] = p_acc[...].astype(BF16)
    p2 = []
    for k in range(1, SIDE):
        at = pl.ds(pl.multiple_of(lax.rem(first + k, SIDE) * quarter, quarter), quarter)
        p2.append(remote(p2_send.at[at, :], p2_recv.at[k - 1], p_sems.at[k], firsts[k - 1]))
        p2[-1].start()

    for hops in (2, 1, 0):
        for way in (0, 1) if hops else (0,):
            project(target(1 - 2 * way, hops))
        if hops == 2:
            z_push(0, 3)
            z_push(1, 3)

    for copy in p2:
        copy.wait()
    at = pl.ds(pl.multiple_of(first * quarter, quarter), quarter)
    part = p_acc[at, :] + sum(p2_recv[k].astype(F32) for k in range(SIDE - 1))
    p_acc[at, :] = part
    p3_send[...] = part.astype(BF16)
    p3 = []
    for k in range(1, SIDE):
        to = pl.ds(pl.multiple_of(lax.rem(second + k, SIDE) * slice_rows, slice_rows), slice_rows)
        p3.append(
            remote(p3_send.at[to, :], p3_recv.at[k - 1], p_sems.at[SIDE + k - 1], seconds[k - 1])
        )
        p3[-1].start()

    z_push(0, 4)
    z_push(1, 4)

    for copy in p3:
        copy.wait()
    start = first * quarter + second * slice_rows
    at = pl.ds(pl.multiple_of(start, slice_rows), slice_rows)
    part = p_acc[at, :] + sum(p3_recv[k].astype(F32) for k in range(SIDE - 1))
    at = pl.ds(pl.multiple_of(mine + start, slice_rows), slice_rows)
    gp_ref[at, :] = part.astype(BF16)
    p4 = []
    for k in range(SIDE - 1):
        p4.append(
            remote(gp_ref.at[at, :], gp_ref.at[at, :], p_sems.at[2 * SIDE - 1 + k], seconds[k])
        )
        p4[-1].start()

    z_push(0, 5)
    z_push(1, 5)

    for copy in p4:
        copy.wait()
    at = pl.ds(pl.multiple_of(mine + first * quarter, quarter), quarter)
    p5 = []
    for k in range(SIDE - 1):
        p5.append(
            remote(gp_ref.at[at, :], gp_ref.at[at, :], p_sems.at[3 * SIDE - 2 + k], firsts[k])
        )
        p5[-1].start()

    z_push(0, 6)
    z_push(1, 6)

    for copy in p5:
        copy.wait()
    at = pl.ds(pl.multiple_of(mine, rows // 2), rows // 2)
    p6 = remote(gp_ref.at[at, :], gp_ref.at[at, :], p_sems.at[4 * SIDE - 3], sibling)
    p6.start()

    for h in (0, 1):
        total = own[z, h * half : (h + 1) * half, :]
        for way in (0, 1):
            for i in (5, 6):
                if piece(way, i)[0] == h:
                    z_copy(way, i).wait_recv()
                    total = total + z_recv[way, i].astype(F32)
        gc_ref[h * half : (h + 1) * half, :] = total.astype(BF16)
    for way in (0, 1):
        for i in range(len(LONG)):
            z_copy(way, i).wait_send()
    p6.wait()


def local(nz, prompts, cands, positive, cot):
    rows, width = prompts.shape
    pool = cands.shape[0]
    block = 256
    chunk = pool // nz
    half = chunk // 2
    quarter = rows // 2 // SIDE
    steps = len(LONG)
    return pl.pallas_call(
        functools.partial(kernel, nz),
        out_shape=(
            jax.ShapeDtypeStruct((rows, width), BF16),
            jax.ShapeDtypeStruct((chunk, width), BF16),
        ),
        in_specs=[pl.BlockSpec(memory_space=pl.ANY)] * 3 + [pl.BlockSpec(memory_space=pltpu.VMEM)],
        out_specs=[pl.BlockSpec(memory_space=pltpu.VMEM)] * 2,
        scratch_shapes=[
            pltpu.VMEM((rows, width), BF16),
            pltpu.VMEM((pool, width), BF16),
            pltpu.VMEM((rows // block, block, pool), jnp.int32),
            pltpu.VMEM((pool, block), F32),
            pltpu.VMEM((pool, block), jnp.int32),
            pltpu.VMEM((pool, rows), BF16),
            pltpu.VMEM((pool, rows), BF16),
            pltpu.VMEM((nz, chunk, width), F32),
            pltpu.VMEM((3, 4, rows), F32),
            pltpu.VMEM((2 * SIDE - 1, 4, rows), F32),
            pltpu.VMEM((2, steps, half, width), BF16),
            pltpu.VMEM((2, steps, half, width), BF16),
            pltpu.VMEM((rows // 2, width), BF16),
            pltpu.VMEM((rows // 2, width), BF16),
            pltpu.VMEM((rows // 2, width), F32),
            pltpu.VMEM((rows // 2, width), BF16),
            pltpu.VMEM((SIDE - 1, quarter, width), BF16),
            pltpu.VMEM((quarter, width), BF16),
            pltpu.VMEM((SIDE - 1, quarter // SIDE, width), BF16),
            pltpu.SemaphoreType.DMA((2 + rows // block,)),
            pltpu.SemaphoreType.DMA((2 * SIDE - 1, 2)),
            pltpu.SemaphoreType.DMA((2, steps, 2)),
            pltpu.SemaphoreType.DMA((4 * SIDE - 2, 2)),
        ],
        compiler_params=pltpu.CompilerParams(
            collective_id=0, has_side_effects=True, vmem_limit_bytes=56 * 1024 * 1024
        ),
    )(prompts, cands, positive, cot.reshape(1, rows))


def solution(mesh):
    placed = (P("prompt", None), P("pool", None), P("prompt", "pool"), P("prompt"))
    return jax.shard_map(
        functools.partial(local, mesh.shape["prompt"]),
        mesh=mesh,
        in_specs=placed,
        out_specs=(P("prompt", None), P(("pool", "prompt"), None)),
        check_vma=False,
    )
```

```python
import functools
import math

import jax
import jax.numpy as jnp
from jax import lax
from jax.experimental import pallas as pl
from jax.experimental.pallas import tpu as pltpu
from jax.sharding import PartitionSpec as P

NEG_FLOOR = -1e30
LOG2E = 1.4426950408889634
F32 = jnp.float32
BF16 = jnp.bfloat16
SIDE = 4
MESH = pl.DeviceIdType.MESH
BLOCK = 256
PARTS = 4
TURNS = 2

ROUTE = [(q, 4) for q in (3, 2)] + [
    (q, hops) for hops in (3, 2, 1) for q in (1, 0, 3, 2)
]
LAG = 4


def kernel(
    nz,
    prompts_hbm,
    cands_hbm,
    positive_hbm,
    cot_ref,
    gp_ref,
    gc_ref,
    prompts,
    cands,
    pos,
    scores,
    pos_t,
    signed,
    weights,
    own,
    raw,
    columns,
    st_send,
    st_recv,
    z_send,
    z_recv,
    p1_send,
    p1_recv,
    p_acc,
    p2_send,
    p2_recv,
    p3_buf,
    load_sem,
    st_sems,
    z_sems,
    p1_sems,
    p2_sems,
    p3_sems,
    p5_sems,
    p6_sems,
):
    rows, width = prompts.shape
    pool = cands.shape[0]
    factor = 2.0 / math.sqrt(width)
    rate = factor * LOG2E
    nblocks = rows // BLOCK
    chunk = pool // nz
    size = chunk // PARTS
    half = rows // 2
    turn = half // TURNS
    share = turn // SIDE

    me = lax.axis_index("pool")
    z = lax.axis_index("prompt")
    core = lax.rem(me, 2)
    x = lax.rem(me // 2, SIDE)
    y = me // (2 * SIDE)
    first = (1 - core) * x + core * y
    second = core * x + (1 - core) * y

    def place(a, b):
        return (((core * a + (1 - core) * b) * SIDE) + (1 - core) * a + core * b) * 2 + core

    sibling = {"pool": me + 1 - 2 * core}
    firsts = [{"pool": place(lax.rem(first + k, SIDE), second)} for k in range(1, SIDE)]
    seconds = [{"pool": place(first, lax.rem(second + k, SIDE))} for k in range(1, SIDE)]
    beside = [{"prompt": lax.rem(z + 1, nz)}, {"prompt": lax.rem(z + nz - 1, nz)}]

    owner = [lax.rem(z + r, nz) for r in range(nz)]

    def spot(r):
        return pl.ds(r * chunk, chunk)

    def source(r):
        return pl.ds(pl.multiple_of(owner[r] * chunk, chunk), chunk)

    load_q = pltpu.make_async_copy(prompts_hbm, prompts, load_sem.at[0])
    load_c = [
        pltpu.make_async_copy(
            cands_hbm.at[source(r), :], cands.at[spot(r), :], load_sem.at[1 + r]
        )
        for r in range(nz)
    ]
    load_p = [
        pltpu.make_async_copy(
            positive_hbm.at[pl.ds(b * BLOCK, BLOCK), :], pos.at[b], load_sem.at[1 + nz + b]
        )
        for b in range(nblocks)
    ]
    load_q.start()
    for load in load_c + load_p:
        load.start()

    barrier = pltpu.get_barrier_semaphore()
    peers = [sibling] + firsts + seconds + beside
    for peer in peers:
        pl.semaphore_signal(barrier, inc=1, device_id=peer, device_id_type=MESH)

    def remote(src, dst, sems, peer):
        return pltpu.make_async_remote_copy(
            src_ref=src,
            dst_ref=dst,
            send_sem=sems.at[0],
            recv_sem=sems.at[1],
            device_id=peer,
            device_id_type=MESH,
        )

    def fold(op, v):
        return op(v.reshape(v.shape[0] // 8, 8, v.shape[1]), axis=0)

    top_all = [None] * nblocks
    top_pos = [None] * nblocks

    def score(b):
        s = lax.dot_general(
            cands[...],
            prompts[pl.ds(b * BLOCK, BLOCK), :],
            (((1,), (1,)), ((), ())),
            preferred_element_type=F32,
        )
        scores[b] = s
        top_all[b] = jnp.max(fold(jnp.max, s), axis=0, keepdims=True)

    def mark(b):
        top = jnp.full((8, BLOCK), NEG_FLOOR, F32)
        for r in range(nz):
            found = pos[b, :, source(r)].T
            pos_t[b % 2, spot(r), :] = found
            kept = jnp.where(found == 1, scores[b, spot(r), :], NEG_FLOOR)
            top = jnp.maximum(top, fold(jnp.max, kept))
        top_pos[b] = jnp.max(top, axis=0, keepdims=True)

    def spread(b):
        cols = pl.ds(b * BLOCK, BLOCK)
        sum_rest = jnp.zeros((8, BLOCK), F32)
        sum_pos = jnp.zeros((8, BLOCK), F32)
        for r in range(nz):
            chosen = pos_t[b % 2, spot(r), :] == 1
            e = jnp.exp2((scores[b, spot(r), :] - jnp.where(chosen, top_pos[b], top_all[b])) * rate)
            rest = jnp.where(chosen, 0.0, e)
            picked = e - rest
            signed[spot(r), cols] = (rest - picked).astype(BF16)
            sum_rest = sum_rest + fold(jnp.sum, rest)
            sum_pos = sum_pos + fold(jnp.sum, picked)
        sum_rest = jnp.sum(sum_rest, axis=0, keepdims=True)
        sum_pos = jnp.sum(sum_pos, axis=0, keepdims=True)
        st_send[0, 0:1, cols] = top_all[b]
        st_send[0, 1:2, cols] = top_pos[b]
        st_send[0, 2:3, cols] = sum_rest + sum_pos * jnp.exp2((top_pos[b] - top_all[b]) * rate)
        st_send[0, 3:4, cols] = sum_pos

    load_q.wait()
    for load in load_c:
        load.wait()
    score(0)
    score(1)
    for b in range(0, nblocks, 2):
        load_p[b].wait()
        load_p[b + 1].wait()
        for c in (b, b + 1):
            if c + 2 < nblocks:
                score(c + 2)
            mark(c)
            spread(c)

    pl.semaphore_wait(barrier, len(peers))

    def merge(parts):
        top = functools.reduce(jnp.maximum, [t[0:2, :] for t in parts])
        total = sum(t[2:4, :] * jnp.exp2((t[0:2, :] - top) * rate) for t in parts)
        return top, total

    def gather(b):
        cols = pl.ds(b * BLOCK, BLOCK)
        e = signed[:, cols]
        zero = jnp.zeros_like(e)
        for kind, part in enumerate((jnp.maximum(e, zero), jnp.minimum(e, zero))):
            raw[kind, cols, :] = lax.dot_general(
                part, cands[...], (((0,), (0,)), ((), ())), preferred_element_type=F32
            )

    swap = remote(st_send.at[0], st_recv.at[0], st_sems.at[0], sibling)
    swap.start()
    swap.wait()
    top, total = merge([st_send.at[0], st_recv.at[0]])
    for stage, group in ((1, firsts), (2, seconds)):
        st_send[stage, 0:2, :] = top
        st_send[stage, 2:4, :] = total
        at = 1 + (stage - 1) * (SIDE - 1)
        copies = [
            remote(st_send.at[stage], st_recv.at[at + k], st_sems.at[at + k], peer)
            for k, peer in enumerate(group)
        ]
        for copy in copies:
            copy.start()
        for b in range((stage - 1) * nblocks // 2, stage * nblocks // 2):
            gather(b)
        for copy in copies:
            copy.wait()
        top, total = merge([st_send.at[stage]] + [st_recv.at[at + k] for k in range(SIDE - 1)])

    local_top = st_send[0, 0:2, :]
    gain = cot_ref[...] * factor
    down = gain * jnp.exp2((local_top - top) * rate) / total
    cross = gain * jnp.exp2((local_top[1:2, :] - top[0:1, :]) * rate) / total[0:1, :]
    scale_rest = down[0:1, :]
    scale_pos = down[1:2, :] - cross

    def project(r):
        e = signed[spot(r), :].astype(F32)
        weights[r] = (e * jnp.where(e < 0.0, scale_pos, scale_rest)).astype(BF16)
        own[r] = jnp.dot(weights[r], prompts[...], preferred_element_type=F32)

    def z_piece(way, i):
        q, hops = ROUTE[i]
        return (q if way == 0 else PARTS - 1 - q), (hops if way == 0 else nz - hops)

    def z_copy(way, i):
        return remote(z_send.at[way, i], z_recv.at[way, i], z_sems.at[way, i], beside[way])

    def z_push(i):
        for way in (0, 1):
            q, r = z_piece(way, i)
            value = own[r, q * size : (q + 1) * size, :]
            if i >= LAG:
                z_copy(way, i - LAG).wait_recv()
                value = value + z_recv[way, i - LAG].astype(F32)
            z_send[way, i] = value.astype(BF16)
            z_copy(way, i).start()

    project(nz // 2)
    z_push(0)
    z_push(1)
    project(3)
    project(nz - 3)
    z_push(2)
    z_push(3)

    lanes = jnp.concatenate(
        [scale_rest, scale_pos, jnp.zeros((6, rows), F32)], axis=0
    )
    columns[:, 0:8] = lanes.T
    mine = core * half

    def scaled(start):
        at = pl.ds(pl.multiple_of(start, turn), turn)
        return raw[0, at, :] * columns[at, 0:1] + raw[1, at, :] * columns[at, 1:2]

    p1 = []
    for u in range(TURNS):
        p1_send[u] = scaled(half - mine + u * turn).astype(BF16)
        p1.append(remote(p1_send.at[u], p1_recv.at[u], p1_sems.at[u], sibling))
        p1[u].start()
    for u in range(TURNS):
        p_acc[u] = scaled(mine + u * turn)

    def my_share(a):
        return pl.ds(pl.multiple_of(a * share, share), share)

    def p2_copy(u, k):
        return remote(
            p2_send.at[u, my_share(lax.rem(first + k + 1, SIDE)), :],
            p2_recv.at[u, k],
            p2_sems.at[u, k],
            firsts[k],
        )

    def p3_copy(u, k):
        return remote(p3_buf.at[u, second], p3_buf.at[u, second], p3_sems.at[u, k], seconds[k])

    def p5_copy(u, k):
        at = pl.ds(pl.multiple_of(mine + u * turn + first * share, share), share)
        return remote(gp_ref.at[at, :], gp_ref.at[at, :], p5_sems.at[u, k], firsts[k])

    def p6_copy(u):
        at = pl.ds(pl.multiple_of(mine + u * turn, turn), turn)
        return remote(gp_ref.at[at, :], gp_ref.at[at, :], p6_sems.at[u], sibling)

    def p2_go(u):
        p1[u].wait()
        value = p_acc[u] + p1_recv[u].astype(F32)
        p_acc[u] = value
        p2_send[u] = value.astype(BF16)
        for k in range(SIDE - 1):
            p2_copy(u, k).start()

    def p3_go(u):
        for k in range(SIDE - 1):
            p2_copy(u, k).wait()
        value = p_acc[u, my_share(first), :] + sum(
            p2_recv[u, k].astype(F32) for k in range(SIDE - 1)
        )
        p3_buf[u, second] = value.astype(BF16)
        for k in range(SIDE - 1):
            p3_copy(u, k).start()

    def p5_go(u):
        for k in range(SIDE - 1):
            p3_copy(u, k).wait()
        value = sum(p3_buf[u, b].astype(F32) for b in range(SIDE))
        at = pl.ds(pl.multiple_of(mine + u * turn + first * share, share), share)
        gp_ref[at, :] = value.astype(BF16)
        for k in range(SIDE - 1):
            p5_copy(u, k).start()

    def p6_go(u):
        for k in range(SIDE - 1):
            p5_copy(u, k).wait()
        p6_copy(u).start()

    project(2)
    p2_go(0)
    p2_go(1)
    z_push(4)
    project(nz - 2)
    z_push(5)
    project(1)
    z_push(6)
    project(nz - 1)
    p3_go(0)
    z_push(7)
    p3_go(1)
    z_push(8)
    project(0)
    z_push(9)
    z_push(10)
    p5_go(0)
    z_push(11)
    p5_go(1)
    z_push(12)
    z_push(13)
    p6_go(0)
    p6_go(1)

    last = len(ROUTE) - LAG
    for i in range(last, len(ROUTE)):
        for way in (0, 1):
            z_copy(way, i).wait_recv()
    for q in range(PARTS):
        value = own[0, q * size : (q + 1) * size, :]
        for i in range(last, len(ROUTE)):
            for way in (0, 1):
                if z_piece(way, i)[0] == q:
                    value = value + z_recv[way, i].astype(F32)
        gc_ref[q * size : (q + 1) * size, :] = value.astype(BF16)
    for i in range(len(ROUTE)):
        for way in (0, 1):
            z_copy(way, i).wait_send()
    for u in range(TURNS):
        p6_copy(u).wait()


def flush(gp, gc, gp_out, gc_out, sems):
    copies = [
        pltpu.make_async_copy(gp, gp_out, sems.at[0]),
        pltpu.make_async_copy(gc, gc_out, sems.at[1]),
    ]
    for copy in copies:
        copy.start()
    for copy in copies:
        copy.wait()


def local(nz, prompts, cands, positive, cot):
    rows, width = prompts.shape
    pool = cands.shape[0]
    nblocks = rows // BLOCK
    chunk = pool // nz
    size = chunk // PARTS
    turn = rows // 2 // TURNS
    share = turn // SIDE
    steps = len(ROUTE)
    dma = pltpu.SemaphoreType.DMA
    results = [((rows, width), BF16), ((chunk, width), BF16)]
    gp, gc = pl.pallas_call(
        functools.partial(kernel, nz),
        out_shape=tuple(pltpu.VMEM(*r) for r in results),
        in_specs=[pl.BlockSpec(memory_space=pl.ANY)] * 3 + [pl.BlockSpec(memory_space=pltpu.VMEM)],
        out_specs=[pl.BlockSpec(memory_space=pltpu.VMEM)] * 2,
        scratch_shapes=[
            pltpu.VMEM((rows, width), BF16),
            pltpu.VMEM((pool, width), BF16),
            pltpu.VMEM((nblocks, BLOCK, pool), jnp.int32),
            pltpu.VMEM((nblocks, pool, BLOCK), F32),
            pltpu.VMEM((2, pool, BLOCK), jnp.int32),
            pltpu.VMEM((pool, rows), BF16),
            pltpu.VMEM((nz, chunk, rows), BF16),
            pltpu.VMEM((nz, chunk, width), F32),
            pltpu.VMEM((2, rows, width), F32),
            pltpu.VMEM((rows, 128), F32),
            pltpu.VMEM((3, 4, rows), F32),
            pltpu.VMEM((2 * SIDE - 1, 4, rows), F32),
            pltpu.VMEM((2, steps, size, width), BF16),
            pltpu.VMEM((2, steps, size, width), BF16),
            pltpu.VMEM((TURNS, turn, width), BF16),
            pltpu.VMEM((TURNS, turn, width), BF16),
            pltpu.VMEM((TURNS, turn, width), F32),
            pltpu.VMEM((TURNS, turn, width), BF16),
            pltpu.VMEM((TURNS, SIDE - 1, share, width), BF16),
            pltpu.VMEM((TURNS, SIDE, share, width), BF16),
            dma((1 + nz + nblocks,)),
            dma((2 * SIDE - 1, 2)),
            dma((2, steps, 2)),
            dma((TURNS, 2)),
            dma((TURNS, SIDE - 1, 2)),
            dma((TURNS, SIDE - 1, 2)),
            dma((TURNS, SIDE - 1, 2)),
            dma((TURNS, 2)),
        ],
        compiler_params=pltpu.CompilerParams(
            collective_id=0, has_side_effects=True, vmem_limit_bytes=56 * 1024 * 1024
        ),
    )(prompts, cands, positive, cot.reshape(1, rows))
    return pl.pallas_call(
        flush,
        out_shape=tuple(jax.ShapeDtypeStruct(*r) for r in results),
        in_specs=[pl.BlockSpec(memory_space=pltpu.VMEM)] * 2,
        out_specs=[pl.BlockSpec(memory_space=pl.ANY)] * 2,
        scratch_shapes=[dma((2,))],
    )(gp, gc)


def solution(mesh):
    placed = (P("prompt", None), P("pool", None), P("prompt", "pool"), P("prompt"))
    return jax.shard_map(
        functools.partial(local, mesh.shape["prompt"]),
        mesh=mesh,
        in_specs=placed,
        out_specs=(P("prompt", None), P(("pool", "prompt"), None)),
        check_vma=False,
    )
```

```python
import functools
import math

import jax
import jax.numpy as jnp
from jax import lax
from jax.experimental import pallas as pl
from jax.experimental.pallas import tpu as pltpu
from jax.sharding import PartitionSpec as P

NEG_FLOOR = -1e30
LOG2E = 1.4426950408889634
F32 = jnp.float32
BF16 = jnp.bfloat16
SIDE = 4
MESH = pl.DeviceIdType.MESH
BLOCK = 256
PARTS = 4
TURNS = 2

ROUTE = [(q, 4) for q in (3, 2)] + [
    (q, hops) for hops in (3, 2, 1) for q in (1, 0, 3, 2)
]
LAG = 4


def kernel(
    nz,
    prompts_hbm,
    cands_hbm,
    positive_hbm,
    cot_ref,
    gp_ref,
    gc_ref,
    prompts,
    cands,
    pos,
    scores,
    pos_t,
    signed,
    weights,
    own,
    raw,
    columns,
    st_send,
    st_recv,
    z_send,
    z_recv,
    p1_send,
    p1_recv,
    p_acc,
    p2_send,
    p2_recv,
    p3_buf,
    load_sem,
    st_sems,
    z_sems,
    p1_sems,
    p2_sems,
    p3_sems,
    p5_sems,
    p6_sems,
):
    rows, width = prompts.shape
    pool = cands.shape[0]
    factor = 2.0 / math.sqrt(width)
    rate = factor * LOG2E
    nblocks = rows // BLOCK
    chunk = pool // nz
    size = chunk // PARTS
    half = rows // 2
    turn = half // TURNS
    share = turn // SIDE

    me = lax.axis_index("pool")
    z = lax.axis_index("prompt")
    core = lax.rem(me, 2)
    x = lax.rem(me // 2, SIDE)
    y = me // (2 * SIDE)
    first = (1 - core) * x + core * y
    second = core * x + (1 - core) * y

    def place(a, b):
        return (((core * a + (1 - core) * b) * SIDE) + (1 - core) * a + core * b) * 2 + core

    sibling = {"pool": me + 1 - 2 * core}
    firsts = [{"pool": place(lax.rem(first + k, SIDE), second)} for k in range(1, SIDE)]
    seconds = [{"pool": place(first, lax.rem(second + k, SIDE))} for k in range(1, SIDE)]
    beside = [{"prompt": lax.rem(z + 1, nz)}, {"prompt": lax.rem(z + nz - 1, nz)}]

    owner = [lax.rem(z + r, nz) for r in range(nz)]

    def spot(r):
        return pl.ds(r * chunk, chunk)

    def source(r):
        return pl.ds(pl.multiple_of(owner[r] * chunk, chunk), chunk)

    load_q = pltpu.make_async_copy(prompts_hbm, prompts, load_sem.at[0])
    load_c = [
        pltpu.make_async_copy(
            cands_hbm.at[source(r), :], cands.at[spot(r), :], load_sem.at[1 + r]
        )
        for r in range(nz)
    ]
    load_p = [
        pltpu.make_async_copy(
            positive_hbm.at[pl.ds(b * BLOCK, BLOCK), :], pos.at[b], load_sem.at[1 + nz + b]
        )
        for b in range(nblocks)
    ]
    load_q.start()
    for load in load_c + load_p:
        load.start()

    barrier = pltpu.get_barrier_semaphore()
    peers = [sibling] + firsts + seconds + beside
    for peer in peers:
        pl.semaphore_signal(barrier, inc=1, device_id=peer, device_id_type=MESH)

    def remote(src, dst, sems, peer):
        return pltpu.make_async_remote_copy(
            src_ref=src,
            dst_ref=dst,
            send_sem=sems.at[0],
            recv_sem=sems.at[1],
            device_id=peer,
            device_id_type=MESH,
        )

    def fold(op, v):
        return op(v.reshape(v.shape[0] // 8, 8, v.shape[1]), axis=0)

    top_all = [None] * nblocks
    top_pos = [None] * nblocks

    def score(b):
        s = lax.dot_general(
            cands[...],
            prompts[pl.ds(b * BLOCK, BLOCK), :],
            (((1,), (1,)), ((), ())),
            preferred_element_type=F32,
        )
        scores[b] = s
        top_all[b] = jnp.max(fold(jnp.max, s), axis=0, keepdims=True)

    def mark(b):
        top = jnp.full((8, BLOCK), NEG_FLOOR, F32)
        for r in range(nz):
            found = pos[b, :, source(r)].T
            pos_t[b % 2, spot(r), :] = found
            kept = jnp.where(found == 1, scores[b, spot(r), :], NEG_FLOOR)
            top = jnp.maximum(top, fold(jnp.max, kept))
        top_pos[b] = jnp.max(top, axis=0, keepdims=True)

    def spread(b):
        cols = pl.ds(b * BLOCK, BLOCK)
        sum_rest = jnp.zeros((8, BLOCK), F32)
        sum_pos = jnp.zeros((8, BLOCK), F32)
        for r in range(nz):
            chosen = pos_t[b % 2, spot(r), :] == 1
            e = jnp.exp2((scores[b, spot(r), :] - jnp.where(chosen, top_pos[b], top_all[b])) * rate)
            rest = jnp.where(chosen, 0.0, e)
            picked = e - rest
            signed[spot(r), cols] = (rest - picked).astype(BF16)
            sum_rest = sum_rest + fold(jnp.sum, rest)
            sum_pos = sum_pos + fold(jnp.sum, picked)
        sum_rest = jnp.sum(sum_rest, axis=0, keepdims=True)
        sum_pos = jnp.sum(sum_pos, axis=0, keepdims=True)
        st_send[0, 0:1, cols] = top_all[b]
        st_send[0, 1:2, cols] = top_pos[b]
        st_send[0, 2:3, cols] = sum_rest + sum_pos * jnp.exp2((top_pos[b] - top_all[b]) * rate)
        st_send[0, 3:4, cols] = sum_pos

    load_q.wait()
    for load in load_c:
        load.wait()
    score(0)
    score(1)
    for b in range(0, nblocks, 2):
        load_p[b].wait()
        load_p[b + 1].wait()
        for c in (b, b + 1):
            if c + 2 < nblocks:
                score(c + 2)
            mark(c)
            spread(c)

    pl.semaphore_wait(barrier, len(peers))

    def merge(parts):
        top = functools.reduce(jnp.maximum, [t[0:2, :] for t in parts])
        total = sum(t[2:4, :] * jnp.exp2((t[0:2, :] - top) * rate) for t in parts)
        return top, total

    def gather(b):
        cols = pl.ds(b * BLOCK, BLOCK)
        e = signed[:, cols]
        zero = jnp.zeros_like(e)
        for kind, part in enumerate((jnp.maximum(e, zero), jnp.minimum(e, zero))):
            raw[kind, cols, :] = lax.dot_general(
                part, cands[...], (((0,), (0,)), ((), ())), preferred_element_type=F32
            )

    swap = remote(st_send.at[0], st_recv.at[0], st_sems.at[0], sibling)
    swap.start()
    swap.wait()
    top, total = merge([st_send.at[0], st_recv.at[0]])
    for stage, group in ((1, firsts), (2, seconds)):
        st_send[stage, 0:2, :] = top
        st_send[stage, 2:4, :] = total
        at = 1 + (stage - 1) * (SIDE - 1)
        copies = [
            remote(st_send.at[stage], st_recv.at[at + k], st_sems.at[at + k], peer)
            for k, peer in enumerate(group)
        ]
        for copy in copies:
            copy.start()
        for b in range((stage - 1) * nblocks // 2, stage * nblocks // 2):
            gather(b)
        for copy in copies:
            copy.wait()
        top, total = merge([st_send.at[stage]] + [st_recv.at[at + k] for k in range(SIDE - 1)])

    local_top = st_send[0, 0:2, :]
    gain = cot_ref[...] * factor
    down = gain * jnp.exp2((local_top - top) * rate) / total
    cross = gain * jnp.exp2((local_top[1:2, :] - top[0:1, :]) * rate) / total[0:1, :]
    scale_rest = down[0:1, :]
    scale_pos = down[1:2, :] - cross

    def project(r):
        e = signed[spot(r), :].astype(F32)
        weights[r] = (e * jnp.where(e < 0.0, scale_pos, scale_rest)).astype(BF16)
        own[r] = jnp.dot(weights[r], prompts[...], preferred_element_type=F32)

    def z_piece(way, i):
        q, hops = ROUTE[i]
        return (q if way == 0 else PARTS - 1 - q), (hops if way == 0 else nz - hops)

    def z_copy(way, i):
        return remote(z_send.at[way, i], z_recv.at[way, i], z_sems.at[way, i], beside[way])

    def z_push(i):
        for way in (0, 1):
            q, r = z_piece(way, i)
            value = own[r, q * size : (q + 1) * size, :]
            if i >= LAG:
                z_copy(way, i - LAG).wait_recv()
                value = value + z_recv[way, i - LAG].astype(F32)
            z_send[way, i] = value.astype(BF16)
            z_copy(way, i).start()

    project(nz // 2)
    z_push(0)
    z_push(1)
    project(3)
    project(nz - 3)
    z_push(2)
    z_push(3)

    lanes = jnp.concatenate(
        [scale_rest, scale_pos, jnp.zeros((6, rows), F32)], axis=0
    )
    columns[:, 0:8] = lanes.T
    mine = core * half

    def scaled(start):
        at = pl.ds(pl.multiple_of(start, turn), turn)
        return raw[0, at, :] * columns[at, 0:1] + raw[1, at, :] * columns[at, 1:2]

    p1 = []
    for u in range(TURNS):
        p1_send[u] = scaled(half - mine + u * turn).astype(BF16)
        p1.append(remote(p1_send.at[u], p1_recv.at[u], p1_sems.at[u], sibling))
        p1[u].start()
    for u in range(TURNS):
        p_acc[u] = scaled(mine + u * turn)

    def my_share(a):
        return pl.ds(pl.multiple_of(a * share, share), share)

    def p2_copy(u, k):
        return remote(
            p2_send.at[u, my_share(lax.rem(first + k + 1, SIDE)), :],
            p2_recv.at[u, k],
            p2_sems.at[u, k],
            firsts[k],
        )

    def p3_copy(u, k):
        return remote(p3_buf.at[u, second], p3_buf.at[u, second], p3_sems.at[u, k], seconds[k])

    def p5_copy(u, k):
        at = pl.ds(pl.multiple_of(mine + u * turn + first * share, share), share)
        return remote(gp_ref.at[at, :], gp_ref.at[at, :], p5_sems.at[u, k], firsts[k])

    def p6_copy(u):
        at = pl.ds(pl.multiple_of(mine + u * turn, turn), turn)
        return remote(gp_ref.at[at, :], gp_ref.at[at, :], p6_sems.at[u], sibling)

    def p2_go(u):
        p1[u].wait()
        value = p_acc[u] + p1_recv[u].astype(F32)
        p_acc[u] = value
        p2_send[u] = value.astype(BF16)
        for k in range(SIDE - 1):
            p2_copy(u, k).start()

    def p3_go(u):
        for k in range(SIDE - 1):
            p2_copy(u, k).wait()
        value = p_acc[u, my_share(first), :] + sum(
            p2_recv[u, k].astype(F32) for k in range(SIDE - 1)
        )
        p3_buf[u, second] = value.astype(BF16)
        for k in range(SIDE - 1):
            p3_copy(u, k).start()

    def p5_go(u):
        for k in range(SIDE - 1):
            p3_copy(u, k).wait()
        value = sum(p3_buf[u, b].astype(F32) for b in range(SIDE))
        at = pl.ds(pl.multiple_of(mine + u * turn + first * share, share), share)
        gp_ref[at, :] = value.astype(BF16)
        for k in range(SIDE - 1):
            p5_copy(u, k).start()

    def p6_go(u):
        for k in range(SIDE - 1):
            p5_copy(u, k).wait()
        p6_copy(u).start()

    project(2)
    p2_go(0)
    p2_go(1)
    z_push(4)
    project(nz - 2)
    z_push(5)
    project(1)
    z_push(6)
    project(nz - 1)
    p3_go(0)
    z_push(7)
    p3_go(1)
    z_push(8)
    project(0)
    z_push(9)
    z_push(10)
    p5_go(0)
    z_push(11)
    p5_go(1)
    z_push(12)
    z_push(13)
    p6_go(0)
    p6_go(1)

    last = len(ROUTE) - LAG
    for i in range(last, len(ROUTE)):
        for way in (0, 1):
            z_copy(way, i).wait_recv()
    for q in range(PARTS):
        value = own[0, q * size : (q + 1) * size, :]
        for i in range(last, len(ROUTE)):
            for way in (0, 1):
                if z_piece(way, i)[0] == q:
                    value = value + z_recv[way, i].astype(F32)
        gc_ref[q * size : (q + 1) * size, :] = value.astype(BF16)
    for i in range(len(ROUTE)):
        for way in (0, 1):
            z_copy(way, i).wait_send()
    for u in range(TURNS):
        p6_copy(u).wait()


def flush(gp, gc, gp_out, gc_out, sems):
    copies = [
        pltpu.make_async_copy(gp, gp_out, sems.at[0]),
        pltpu.make_async_copy(gc, gc_out, sems.at[1]),
    ]
    for copy in copies:
        copy.start()
    for copy in copies:
        copy.wait()


def local(nz, prompts, cands, positive, cot):
    rows, width = prompts.shape
    pool = cands.shape[0]
    nblocks = rows // BLOCK
    chunk = pool // nz
    size = chunk // PARTS
    turn = rows // 2 // TURNS
    share = turn // SIDE
    steps = len(ROUTE)
    dma = pltpu.SemaphoreType.DMA
    results = [((rows, width), BF16), ((chunk, width), BF16)]
    gp, gc = pl.pallas_call(
        functools.partial(kernel, nz),
        out_shape=tuple(pltpu.VMEM(*r) for r in results),
        in_specs=[pl.BlockSpec(memory_space=pl.ANY)] * 3 + [pl.BlockSpec(memory_space=pltpu.VMEM)],
        out_specs=[pl.BlockSpec(memory_space=pltpu.VMEM)] * 2,
        scratch_shapes=[
            pltpu.VMEM((rows, width), BF16),
            pltpu.VMEM((pool, width), BF16),
            pltpu.VMEM((nblocks, BLOCK, pool), jnp.int32),
            pltpu.VMEM((nblocks, pool, BLOCK), F32),
            pltpu.VMEM((2, pool, BLOCK), jnp.int32),
            pltpu.VMEM((pool, rows), BF16),
            pltpu.VMEM((nz, chunk, rows), BF16),
            pltpu.VMEM((nz, chunk, width), F32),
            pltpu.VMEM((2, rows, width), F32),
            pltpu.VMEM((rows, 128), F32),
            pltpu.VMEM((3, 4, rows), F32),
            pltpu.VMEM((2 * SIDE - 1, 4, rows), F32),
            pltpu.VMEM((2, steps, size, width), BF16),
            pltpu.VMEM((2, steps, size, width), BF16),
            pltpu.VMEM((TURNS, turn, width), BF16),
            pltpu.VMEM((TURNS, turn, width), BF16),
            pltpu.VMEM((TURNS, turn, width), F32),
            pltpu.VMEM((TURNS, turn, width), BF16),
            pltpu.VMEM((TURNS, SIDE - 1, share, width), BF16),
            pltpu.VMEM((TURNS, SIDE, share, width), BF16),
            dma((1 + nz + nblocks,)),
            dma((2 * SIDE - 1, 2)),
            dma((2, steps, 2)),
            dma((TURNS, 2)),
            dma((TURNS, SIDE - 1, 2)),
            dma((TURNS, SIDE - 1, 2)),
            dma((TURNS, SIDE - 1, 2)),
            dma((TURNS, 2)),
        ],
        compiler_params=pltpu.CompilerParams(
            collective_id=0, has_side_effects=True, vmem_limit_bytes=56 * 1024 * 1024
        ),
    )(prompts, cands, positive, cot.reshape(1, rows))
    return pl.pallas_call(
        flush,
        out_shape=tuple(jax.ShapeDtypeStruct(*r) for r in results),
        in_specs=[pl.BlockSpec(memory_space=pl.ANY)] * 2,
        out_specs=[pl.BlockSpec(memory_space=pl.ANY)] * 2,
        scratch_shapes=[dma((2,))],
        compiler_params=pltpu.CompilerParams(vmem_limit_bytes=1024 * 1024),
    )(gp, gc)


def solution(mesh):
    placed = (P("prompt", None), P("pool", None), P("prompt", "pool"), P("prompt"))
    return jax.shard_map(
        functools.partial(local, mesh.shape["prompt"]),
        mesh=mesh,
        in_specs=placed,
        out_specs=(P("prompt", None), P(("pool", "prompt"), None)),
        check_vma=False,
    )
```

```python
import functools
import math

import jax
import jax.numpy as jnp
from jax import lax
from jax.experimental import pallas as pl
from jax.experimental.pallas import tpu as pltpu
from jax.sharding import PartitionSpec as P

NEG_FLOOR = -1e30
LOG2E = 1.4426950408889634
F32 = jnp.float32
BF16 = jnp.bfloat16
SIDE = 4
MESH = pl.DeviceIdType.MESH
BLOCK = 256
PARTS = 2
TURNS = 2

ROUTE = [(1, 4)] + [(q, hops) for hops in (3, 2, 1) for q in (0, 1)]
LAG = 2


def kernel(
    nz,
    prompts_hbm,
    cands_hbm,
    positive_hbm,
    cot_hbm,
    gp_ref,
    gc_ref,
    prompts,
    cands,
    cot,
    pos,
    scores,
    pos_t,
    signed,
    weights,
    own,
    raw,
    columns,
    st_send,
    st_recv,
    z_send,
    z_recv,
    p1_send,
    p1_recv,
    p_acc,
    p2_send,
    p2_recv,
    p3_buf,
    load_sem,
    st_sems,
    z_sems,
    p1_sems,
    p2_sems,
    p3_sems,
    p5_sems,
    p6_sems,
):
    rows, width = prompts.shape
    pool = cands.shape[0]
    factor = 2.0 / math.sqrt(width)
    rate = factor * LOG2E
    nblocks = rows // BLOCK
    chunk = pool // nz
    size = chunk // PARTS
    half = rows // 2
    turn = half // TURNS
    share = turn // SIDE

    me = lax.axis_index("pool")
    z = lax.axis_index("prompt")
    core = lax.rem(me, 2)
    x = lax.rem(me // 2, SIDE)
    y = me // (2 * SIDE)
    first = (1 - core) * x + core * y
    second = core * x + (1 - core) * y

    def place(a, b):
        return (((core * a + (1 - core) * b) * SIDE) + (1 - core) * a + core * b) * 2 + core

    sibling = {"pool": me + 1 - 2 * core}
    firsts = [{"pool": place(lax.rem(first + k, SIDE), second)} for k in range(1, SIDE)]
    seconds = [{"pool": place(first, lax.rem(second + k, SIDE))} for k in range(1, SIDE)]
    beside = [{"prompt": lax.rem(z + 1, nz)}, {"prompt": lax.rem(z + nz - 1, nz)}]

    owner = [lax.rem(z + r, nz) for r in range(nz)]

    def spot(r):
        return pl.ds(r * chunk, chunk)

    def source(r):
        return pl.ds(pl.multiple_of(owner[r] * chunk, chunk), chunk)

    load_q = pltpu.make_async_copy(prompts_hbm, prompts, load_sem.at[0])
    load_c = [
        pltpu.make_async_copy(
            cands_hbm.at[source(r), :], cands.at[spot(r), :], load_sem.at[1 + r]
        )
        for r in range(nz)
    ]
    load_p = [
        pltpu.make_async_copy(
            positive_hbm.at[pl.ds(b * BLOCK, BLOCK), :], pos.at[b], load_sem.at[1 + nz + b]
        )
        for b in range(nblocks)
    ]
    load_cot = pltpu.make_async_copy(cot_hbm, cot, load_sem.at[1 + nz + nblocks])
    load_q.start()
    for load in load_c + load_p + [load_cot]:
        load.start()

    barrier = pltpu.get_barrier_semaphore()
    peers = [sibling] + firsts + seconds + beside
    for peer in peers:
        pl.semaphore_signal(barrier, inc=1, device_id=peer, device_id_type=MESH)

    def remote(src, dst, sems, peer):
        return pltpu.make_async_remote_copy(
            src_ref=src,
            dst_ref=dst,
            send_sem=sems.at[0],
            recv_sem=sems.at[1],
            device_id=peer,
            device_id_type=MESH,
        )

    def fold(op, v):
        return op(v.reshape(v.shape[0] // 8, 8, v.shape[1]), axis=0)

    top_all = [None] * nblocks
    top_pos = [None] * nblocks

    def score(b):
        s = lax.dot_general(
            cands[...],
            prompts[pl.ds(b * BLOCK, BLOCK), :],
            (((1,), (1,)), ((), ())),
            preferred_element_type=F32,
        )
        scores[b] = s
        top_all[b] = jnp.max(fold(jnp.max, s), axis=0, keepdims=True)

    def mark(b):
        top = jnp.full((8, BLOCK), NEG_FLOOR, F32)
        for r in range(nz):
            found = pos[b, :, source(r)].T
            pos_t[b % 2, spot(r), :] = found
            kept = jnp.where(found == 1, scores[b, spot(r), :], NEG_FLOOR)
            top = jnp.maximum(top, fold(jnp.max, kept))
        top_pos[b] = jnp.max(top, axis=0, keepdims=True)

    def spread(b):
        cols = pl.ds(b * BLOCK, BLOCK)
        sum_rest = jnp.zeros((8, BLOCK), F32)
        sum_pos = jnp.zeros((8, BLOCK), F32)
        for r in range(nz):
            chosen = pos_t[b % 2, spot(r), :] == 1
            e = jnp.exp2((scores[b, spot(r), :] - jnp.where(chosen, top_pos[b], top_all[b])) * rate)
            rest = jnp.where(chosen, 0.0, e)
            picked = e - rest
            signed[spot(r), cols] = (rest - picked).astype(BF16)
            sum_rest = sum_rest + fold(jnp.sum, rest)
            sum_pos = sum_pos + fold(jnp.sum, picked)
        sum_rest = jnp.sum(sum_rest, axis=0, keepdims=True)
        sum_pos = jnp.sum(sum_pos, axis=0, keepdims=True)
        st_send[0, 0:1, cols] = top_all[b]
        st_send[0, 1:2, cols] = top_pos[b]
        st_send[0, 2:3, cols] = sum_rest + sum_pos * jnp.exp2((top_pos[b] - top_all[b]) * rate)
        st_send[0, 3:4, cols] = sum_pos

    load_q.wait()
    for load in load_c:
        load.wait()
    score(0)
    score(1)
    for b in range(0, nblocks, 2):
        load_p[b].wait()
        load_p[b + 1].wait()
        for c in (b, b + 1):
            if c + 2 < nblocks:
                score(c + 2)
            mark(c)
            spread(c)

    pl.semaphore_wait(barrier, len(peers))

    def merge(parts):
        top = functools.reduce(jnp.maximum, [t[0:2, :] for t in parts])
        total = sum(t[2:4, :] * jnp.exp2((t[0:2, :] - top) * rate) for t in parts)
        return top, total

    def gather(b):
        cols = pl.ds(b * BLOCK, BLOCK)
        e = signed[:, cols]
        zero = jnp.zeros_like(e)
        for kind, part in enumerate((jnp.maximum(e, zero), jnp.minimum(e, zero))):
            raw[kind, cols, :] = lax.dot_general(
                part, cands[...], (((0,), (0,)), ((), ())), preferred_element_type=F32
            )

    swap = remote(st_send.at[0], st_recv.at[0], st_sems.at[0], sibling)
    swap.start()
    swap.wait()
    top, total = merge([st_send.at[0], st_recv.at[0]])
    for stage, group in ((1, firsts), (2, seconds)):
        st_send[stage, 0:2, :] = top
        st_send[stage, 2:4, :] = total
        at = 1 + (stage - 1) * (SIDE - 1)
        copies = [
            remote(st_send.at[stage], st_recv.at[at + k], st_sems.at[at + k], peer)
            for k, peer in enumerate(group)
        ]
        for copy in copies:
            copy.start()
        for b in range((stage - 1) * nblocks // 2, stage * nblocks // 2):
            gather(b)
        for copy in copies:
            copy.wait()
        top, total = merge([st_send.at[stage]] + [st_recv.at[at + k] for k in range(SIDE - 1)])

    local_top = st_send[0, 0:2, :]
    load_cot.wait()
    gain = cot[...] * factor
    down = gain * jnp.exp2((local_top - top) * rate) / total
    cross = gain * jnp.exp2((local_top[1:2, :] - top[0:1, :]) * rate) / total[0:1, :]
    scale_rest = down[0:1, :]
    scale_pos = down[1:2, :] - cross

    def project(r):
        e = signed[spot(r), :].astype(F32)
        weights[r] = (e * jnp.where(e < 0.0, scale_pos, scale_rest)).astype(BF16)
        own[r] = jnp.dot(weights[r], prompts[...], preferred_element_type=F32)

    def z_piece(way, i):
        q, hops = ROUTE[i]
        return (q if way == 0 else PARTS - 1 - q), (hops if way == 0 else nz - hops)

    def z_copy(way, i):
        return remote(z_send.at[way, i], z_recv.at[way, i], z_sems.at[way, i], beside[way])

    def z_push(i):
        for way in (0, 1):
            q, r = z_piece(way, i)
            value = own[r, q * size : (q + 1) * size, :]
            if i >= LAG:
                z_copy(way, i - LAG).wait_recv()
                value = value + z_recv[way, i - LAG].astype(F32)
            z_send[way, i] = value.astype(BF16)
            z_copy(way, i).start()

    project(nz // 2)
    z_push(0)
    project(3)
    project(nz - 3)
    z_push(1)

    lanes = jnp.concatenate(
        [scale_rest, scale_pos, jnp.zeros((6, rows), F32)], axis=0
    )
    columns[:, 0:8] = lanes.T
    mine = core * half

    def scaled(start):
        at = pl.ds(pl.multiple_of(start, turn), turn)
        return raw[0, at, :] * columns[at, 0:1] + raw[1, at, :] * columns[at, 1:2]

    p1 = []
    for u in range(TURNS):
        p1_send[u] = scaled(half - mine + u * turn).astype(BF16)
        p1.append(remote(p1_send.at[u], p1_recv.at[u], p1_sems.at[u], sibling))
        p1[u].start()
    for u in range(TURNS):
        p_acc[u] = scaled(mine + u * turn)

    def my_share(a):
        return pl.ds(pl.multiple_of(a * share, share), share)

    def p2_copy(u, k):
        return remote(
            p2_send.at[u, my_share(lax.rem(first + k + 1, SIDE)), :],
            p2_recv.at[u, k],
            p2_sems.at[u, k],
            firsts[k],
        )

    def p3_copy(u, k):
        return remote(p3_buf.at[u, second], p3_buf.at[u, second], p3_sems.at[u, k], seconds[k])

    def p5_copy(u, k):
        at = pl.ds(pl.multiple_of(mine + u * turn + first * share, share), share)
        return remote(gp_ref.at[at, :], gp_ref.at[at, :], p5_sems.at[u, k], firsts[k])

    def p6_copy(u):
        at = pl.ds(pl.multiple_of(mine + u * turn, turn), turn)
        return remote(gp_ref.at[at, :], gp_ref.at[at, :], p6_sems.at[u], sibling)

    def p2_go(u):
        p1[u].wait()
        value = p_acc[u] + p1_recv[u].astype(F32)
        p_acc[u] = value
        p2_send[u] = value.astype(BF16)
        for k in range(SIDE - 1):
            p2_copy(u, k).start()

    def p3_go(u):
        for k in range(SIDE - 1):
            p2_copy(u, k).wait()
        value = p_acc[u, my_share(first), :] + sum(
            p2_recv[u, k].astype(F32) for k in range(SIDE - 1)
        )
        p3_buf[u, second] = value.astype(BF16)
        for k in range(SIDE - 1):
            p3_copy(u, k).start()

    def p5_go(u):
        for k in range(SIDE - 1):
            p3_copy(u, k).wait()
        value = sum(p3_buf[u, b].astype(F32) for b in range(SIDE))
        at = pl.ds(pl.multiple_of(mine + u * turn + first * share, share), share)
        gp_ref[at, :] = value.astype(BF16)
        for k in range(SIDE - 1):
            p5_copy(u, k).start()

    def p6_go(u):
        for k in range(SIDE - 1):
            p5_copy(u, k).wait()
        p6_copy(u).start()

    project(2)
    p2_go(0)
    p2_go(1)
    project(nz - 2)
    z_push(2)
    project(1)
    p3_go(0)
    z_push(3)
    p3_go(1)
    project(nz - 1)
    z_push(4)
    project(0)
    p5_go(0)
    z_push(5)
    p5_go(1)
    z_push(6)
    p6_go(0)
    p6_go(1)

    last = len(ROUTE) - LAG
    for i in range(last, len(ROUTE)):
        for way in (0, 1):
            z_copy(way, i).wait_recv()
    for q in range(PARTS):
        value = own[0, q * size : (q + 1) * size, :]
        for i in range(last, len(ROUTE)):
            for way in (0, 1):
                if z_piece(way, i)[0] == q:
                    value = value + z_recv[way, i].astype(F32)
        gc_ref[q * size : (q + 1) * size, :] = value.astype(BF16)
    for i in range(len(ROUTE)):
        for way in (0, 1):
            z_copy(way, i).wait_send()
    for u in range(TURNS):
        p6_copy(u).wait()


def flush(gp, gc, gp_out, gc_out, sems):
    copies = [
        pltpu.make_async_copy(gp, gp_out, sems.at[0]),
        pltpu.make_async_copy(gc, gc_out, sems.at[1]),
    ]
    for copy in copies:
        copy.start()
    for copy in copies:
        copy.wait()


def local(nz, prompts, cands, positive, cot):
    rows, width = prompts.shape
    pool = cands.shape[0]
    nblocks = rows // BLOCK
    chunk = pool // nz
    size = chunk // PARTS
    turn = rows // 2 // TURNS
    share = turn // SIDE
    steps = len(ROUTE)
    dma = pltpu.SemaphoreType.DMA
    results = [((rows, width), BF16), ((chunk, width), BF16)]
    gp, gc = pl.pallas_call(
        functools.partial(kernel, nz),
        out_shape=tuple(pltpu.VMEM(*r) for r in results),
        in_specs=[pl.BlockSpec(memory_space=pl.ANY)] * 4,
        out_specs=[pl.BlockSpec(memory_space=pltpu.VMEM)] * 2,
        scratch_shapes=[
            pltpu.VMEM((rows, width), BF16),
            pltpu.VMEM((pool, width), BF16),
            pltpu.VMEM((1, rows), F32),
            pltpu.VMEM((nblocks, BLOCK, pool), jnp.int32),
            pltpu.VMEM((nblocks, pool, BLOCK), F32),
            pltpu.VMEM((2, pool, BLOCK), jnp.int32),
            pltpu.VMEM((pool, rows), BF16),
            pltpu.VMEM((nz, chunk, rows), BF16),
            pltpu.VMEM((nz, chunk, width), F32),
            pltpu.VMEM((2, rows, width), F32),
            pltpu.VMEM((rows, 128), F32),
            pltpu.VMEM((3, 4, rows), F32),
            pltpu.VMEM((2 * SIDE - 1, 4, rows), F32),
            pltpu.VMEM((2, steps, size, width), BF16),
            pltpu.VMEM((2, steps, size, width), BF16),
            pltpu.VMEM((TURNS, turn, width), BF16),
            pltpu.VMEM((TURNS, turn, width), BF16),
            pltpu.VMEM((TURNS, turn, width), F32),
            pltpu.VMEM((TURNS, turn, width), BF16),
            pltpu.VMEM((TURNS, SIDE - 1, share, width), BF16),
            pltpu.VMEM((TURNS, SIDE, share, width), BF16),
            dma((2 + nz + nblocks,)),
            dma((2 * SIDE - 1, 2)),
            dma((2, steps, 2)),
            dma((TURNS, 2)),
            dma((TURNS, SIDE - 1, 2)),
            dma((TURNS, SIDE - 1, 2)),
            dma((TURNS, SIDE - 1, 2)),
            dma((TURNS, 2)),
        ],
        compiler_params=pltpu.CompilerParams(
            collective_id=0, has_side_effects=True, vmem_limit_bytes=56 * 1024 * 1024
        ),
    )(prompts, cands, positive, cot.reshape(1, rows))
    return pl.pallas_call(
        flush,
        out_shape=tuple(jax.ShapeDtypeStruct(*r) for r in results),
        in_specs=[pl.BlockSpec(memory_space=pl.ANY)] * 2,
        out_specs=[pl.BlockSpec(memory_space=pl.ANY)] * 2,
        scratch_shapes=[dma((2,))],
        compiler_params=pltpu.CompilerParams(vmem_limit_bytes=1024 * 1024),
    )(gp, gc)


def solution(mesh):
    placed = (P("prompt", None), P("pool", None), P("prompt", "pool"), P("prompt"))
    return jax.shard_map(
        functools.partial(local, mesh.shape["prompt"]),
        mesh=mesh,
        in_specs=placed,
        out_specs=(P("prompt", None), P(("pool", "prompt"), None)),
        check_vma=False,
    )
```

```python
import functools
import math

import jax
import jax.numpy as jnp
from jax import lax
from jax.experimental import pallas as pl
from jax.experimental.pallas import tpu as pltpu
from jax.sharding import PartitionSpec as P

NEG_FLOOR = -1e30
LOG2E = 1.4426950408889634
F32 = jnp.float32
BF16 = jnp.bfloat16
SIDE = 4
SHIFTS = (2, 1, 3)
MESH = pl.DeviceIdType.MESH
BLOCK = 256
PARTS = 2
TURNS = 2

ROUTE = [(1, 4)] + [(q, hops) for hops in (3, 2, 1) for q in (0, 1)]
LAG = 2


def kernel(
    nz,
    prompts_hbm,
    cands_hbm,
    positive_hbm,
    cot_hbm,
    gp_ref,
    gc_ref,
    prompts,
    cands,
    cot,
    pos,
    scores,
    pos_t,
    signed,
    weights,
    own,
    raw,
    columns,
    st_send,
    st_recv,
    z_send,
    z_recv,
    p1_send,
    p1_recv,
    p_acc,
    p2_send,
    p2_recv,
    p3_buf,
    load_sem,
    st_sems,
    z_sems,
    p1_sems,
    p2_sems,
    p3_sems,
    p5_sems,
    p6_sems,
):
    rows, width = prompts.shape
    pool = cands.shape[0]
    factor = 2.0 / math.sqrt(width)
    rate = factor * LOG2E
    nblocks = rows // BLOCK
    chunk = pool // nz
    size = chunk // PARTS
    half = rows // 2
    turn = half // TURNS
    share = turn // SIDE

    me = lax.axis_index("pool")
    z = lax.axis_index("prompt")
    core = lax.rem(me, 2)
    x = lax.rem(me // 2, SIDE)
    y = me // (2 * SIDE)
    first = (1 - core) * x + core * y
    second = core * x + (1 - core) * y

    def place(a, b):
        return (((core * a + (1 - core) * b) * SIDE) + (1 - core) * a + core * b) * 2 + core

    sibling = {"pool": me + 1 - 2 * core}
    firsts = [{"pool": place(lax.rem(first + k, SIDE), second)} for k in SHIFTS]
    seconds = [{"pool": place(first, lax.rem(second + k, SIDE))} for k in SHIFTS]
    beside = [{"prompt": lax.rem(z + 1, nz)}, {"prompt": lax.rem(z + nz - 1, nz)}]

    owner = [lax.rem(z + r, nz) for r in range(nz)]

    def spot(r):
        return pl.ds(r * chunk, chunk)

    def source(r):
        return pl.ds(pl.multiple_of(owner[r] * chunk, chunk), chunk)

    load_q = pltpu.make_async_copy(prompts_hbm, prompts, load_sem.at[0])
    load_c = [
        pltpu.make_async_copy(
            cands_hbm.at[source(r), :], cands.at[spot(r), :], load_sem.at[1 + r]
        )
        for r in range(nz)
    ]
    load_p = [
        pltpu.make_async_copy(
            positive_hbm.at[pl.ds(b * BLOCK, BLOCK), :], pos.at[b], load_sem.at[1 + nz + b]
        )
        for b in range(nblocks)
    ]
    load_cot = pltpu.make_async_copy(cot_hbm, cot, load_sem.at[1 + nz + nblocks])
    load_q.start()
    for load in load_c + load_p + [load_cot]:
        load.start()

    barrier = pltpu.get_barrier_semaphore()
    peers = [sibling] + firsts + seconds + beside
    for peer in peers:
        pl.semaphore_signal(barrier, inc=1, device_id=peer, device_id_type=MESH)

    def remote(src, dst, sems, peer):
        return pltpu.make_async_remote_copy(
            src_ref=src,
            dst_ref=dst,
            send_sem=sems.at[0],
            recv_sem=sems.at[1],
            device_id=peer,
            device_id_type=MESH,
        )

    def fold(op, v):
        return op(v.reshape(v.shape[0] // 8, 8, v.shape[1]), axis=0)

    top_all = [None] * nblocks
    top_pos = [None] * nblocks

    def score(b):
        s = lax.dot_general(
            cands[...],
            prompts[pl.ds(b * BLOCK, BLOCK), :],
            (((1,), (1,)), ((), ())),
            preferred_element_type=F32,
        )
        scores[b] = s
        top_all[b] = jnp.max(fold(jnp.max, s), axis=0, keepdims=True)

    def mark(b):
        top = jnp.full((8, BLOCK), NEG_FLOOR, F32)
        for r in range(nz):
            found = pos[b, :, source(r)].T
            pos_t[b % 2, spot(r), :] = found
            kept = jnp.where(found == 1, scores[b, spot(r), :], NEG_FLOOR)
            top = jnp.maximum(top, fold(jnp.max, kept))
        top_pos[b] = jnp.max(top, axis=0, keepdims=True)

    def spread(b):
        cols = pl.ds(b * BLOCK, BLOCK)
        sum_rest = jnp.zeros((8, BLOCK), F32)
        sum_pos = jnp.zeros((8, BLOCK), F32)
        for r in range(nz):
            chosen = pos_t[b % 2, spot(r), :] == 1
            e = jnp.exp2((scores[b, spot(r), :] - jnp.where(chosen, top_pos[b], top_all[b])) * rate)
            rest = jnp.where(chosen, 0.0, e)
            picked = e - rest
            signed[spot(r), cols] = (rest - picked).astype(BF16)
            sum_rest = sum_rest + fold(jnp.sum, rest)
            sum_pos = sum_pos + fold(jnp.sum, picked)
        sum_rest = jnp.sum(sum_rest, axis=0, keepdims=True)
        sum_pos = jnp.sum(sum_pos, axis=0, keepdims=True)
        st_send[0, 0:1, cols] = top_all[b]
        st_send[0, 1:2, cols] = top_pos[b]
        st_send[0, 2:3, cols] = sum_rest + sum_pos * jnp.exp2((top_pos[b] - top_all[b]) * rate)
        st_send[0, 3:4, cols] = sum_pos

    load_q.wait()
    for load in load_c:
        load.wait()
    score(0)
    score(1)
    for b in range(0, nblocks, 2):
        load_p[b].wait()
        load_p[b + 1].wait()
        for c in (b, b + 1):
            if c + 2 < nblocks:
                score(c + 2)
            mark(c)
            spread(c)

    pl.semaphore_wait(barrier, len(peers))

    def merge(parts):
        top = functools.reduce(jnp.maximum, [t[0:2, :] for t in parts])
        total = sum(t[2:4, :] * jnp.exp2((t[0:2, :] - top) * rate) for t in parts)
        return top, total

    def gather(b):
        cols = pl.ds(b * BLOCK, BLOCK)
        e = signed[:, cols]
        zero = jnp.zeros_like(e)
        for kind, part in enumerate((jnp.maximum(e, zero), jnp.minimum(e, zero))):
            raw[kind, cols, :] = lax.dot_general(
                part, cands[...], (((0,), (0,)), ((), ())), preferred_element_type=F32
            )

    swap = remote(st_send.at[0], st_recv.at[0], st_sems.at[0], sibling)
    swap.start()
    swap.wait()
    top, total = merge([st_send.at[0], st_recv.at[0]])
    for stage, group in ((1, firsts), (2, seconds)):
        st_send[stage, 0:2, :] = top
        st_send[stage, 2:4, :] = total
        at = 1 + (stage - 1) * (SIDE - 1)
        copies = [
            remote(st_send.at[stage], st_recv.at[at + k], st_sems.at[at + k], peer)
            for k, peer in enumerate(group)
        ]
        for copy in copies:
            copy.start()
        for b in range((stage - 1) * nblocks // 2, stage * nblocks // 2):
            gather(b)
        for copy in copies:
            copy.wait()
        top, total = merge([st_send.at[stage]] + [st_recv.at[at + k] for k in range(SIDE - 1)])

    local_top = st_send[0, 0:2, :]
    load_cot.wait()
    gain = cot[...] * factor
    down = gain * jnp.exp2((local_top - top) * rate) / total
    cross = gain * jnp.exp2((local_top[1:2, :] - top[0:1, :]) * rate) / total[0:1, :]
    scale_rest = down[0:1, :]
    scale_pos = down[1:2, :] - cross

    def project(r):
        e = signed[spot(r), :].astype(F32)
        weights[r] = (e * jnp.where(e < 0.0, scale_pos, scale_rest)).astype(BF16)
        own[r] = jnp.dot(weights[r], prompts[...], preferred_element_type=F32)

    def z_piece(way, i):
        q, hops = ROUTE[i]
        return (q if way == 0 else PARTS - 1 - q), (hops if way == 0 else nz - hops)

    def z_copy(way, i):
        return remote(z_send.at[way, i], z_recv.at[way, i], z_sems.at[way, i], beside[way])

    def z_push(i):
        for way in (0, 1):
            q, r = z_piece(way, i)
            value = own[r, q * size : (q + 1) * size, :]
            if i >= LAG:
                z_copy(way, i - LAG).wait_recv()
                value = value + z_recv[way, i - LAG].astype(F32)
            z_send[way, i] = value.astype(BF16)
            z_copy(way, i).start()

    project(nz // 2)
    z_push(0)
    project(3)
    project(nz - 3)
    z_push(1)

    lanes = jnp.concatenate(
        [scale_rest, scale_pos, jnp.zeros((6, rows), F32)], axis=0
    )
    columns[:, 0:8] = lanes.T
    mine = core * half

    def scaled(start):
        at = pl.ds(pl.multiple_of(start, turn), turn)
        return raw[0, at, :] * columns[at, 0:1] + raw[1, at, :] * columns[at, 1:2]

    p1 = []
    for u in range(TURNS):
        p1_send[u] = scaled(half - mine + u * turn).astype(BF16)
        p1.append(remote(p1_send.at[u], p1_recv.at[u], p1_sems.at[u], sibling))
        p1[u].start()
    for u in range(TURNS):
        p_acc[u] = scaled(mine + u * turn)

    def my_share(a):
        return pl.ds(pl.multiple_of(a * share, share), share)

    def p2_copy(u, k):
        return remote(
            p2_send.at[u, my_share(lax.rem(first + SHIFTS[k], SIDE)), :],
            p2_recv.at[u, k],
            p2_sems.at[u, k],
            firsts[k],
        )

    def p3_copy(u, k):
        return remote(p3_buf.at[u, second], p3_buf.at[u, second], p3_sems.at[u, k], seconds[k])

    def p5_copy(u, k):
        at = pl.ds(pl.multiple_of(mine + u * turn + first * share, share), share)
        return remote(gp_ref.at[at, :], gp_ref.at[at, :], p5_sems.at[u, k], firsts[k])

    def p6_copy(u):
        at = pl.ds(pl.multiple_of(mine + u * turn, turn), turn)
        return remote(gp_ref.at[at, :], gp_ref.at[at, :], p6_sems.at[u], sibling)

    def p2_go(u):
        p1[u].wait()
        value = p_acc[u] + p1_recv[u].astype(F32)
        p_acc[u] = value
        p2_send[u] = value.astype(BF16)
        for k in range(SIDE - 1):
            p2_copy(u, k).start()

    def p3_go(u):
        for k in range(SIDE - 1):
            p2_copy(u, k).wait()
        value = p_acc[u, my_share(first), :] + sum(
            p2_recv[u, k].astype(F32) for k in range(SIDE - 1)
        )
        p3_buf[u, second] = value.astype(BF16)
        for k in range(SIDE - 1):
            p3_copy(u, k).start()

    def p5_go(u):
        for k in range(SIDE - 1):
            p3_copy(u, k).wait()
        value = sum(p3_buf[u, b].astype(F32) for b in range(SIDE))
        at = pl.ds(pl.multiple_of(mine + u * turn + first * share, share), share)
        gp_ref[at, :] = value.astype(BF16)
        for k in range(SIDE - 1):
            p5_copy(u, k).start()

    def p6_go(u):
        for k in range(SIDE - 1):
            p5_copy(u, k).wait()
        p6_copy(u).start()

    project(2)
    p2_go(0)
    p2_go(1)
    project(nz - 2)
    z_push(2)
    project(1)
    p3_go(0)
    z_push(3)
    p3_go(1)
    project(nz - 1)
    z_push(4)
    project(0)
    p5_go(0)
    z_push(5)
    p5_go(1)
    z_push(6)
    p6_go(0)
    p6_go(1)

    last = len(ROUTE) - LAG
    for i in range(last, len(ROUTE)):
        for way in (0, 1):
            z_copy(way, i).wait_recv()
    for q in range(PARTS):
        value = own[0, q * size : (q + 1) * size, :]
        for i in range(last, len(ROUTE)):
            for way in (0, 1):
                if z_piece(way, i)[0] == q:
                    value = value + z_recv[way, i].astype(F32)
        gc_ref[q * size : (q + 1) * size, :] = value.astype(BF16)
    for i in range(len(ROUTE)):
        for way in (0, 1):
            z_copy(way, i).wait_send()
    for u in range(TURNS):
        p6_copy(u).wait()


def flush(gp, gc, gp_out, gc_out, sems):
    copies = [
        pltpu.make_async_copy(gp, gp_out, sems.at[0]),
        pltpu.make_async_copy(gc, gc_out, sems.at[1]),
    ]
    for copy in copies:
        copy.start()
    for copy in copies:
        copy.wait()


def local(nz, prompts, cands, positive, cot):
    rows, width = prompts.shape
    pool = cands.shape[0]
    nblocks = rows // BLOCK
    chunk = pool // nz
    size = chunk // PARTS
    turn = rows // 2 // TURNS
    share = turn // SIDE
    steps = len(ROUTE)
    dma = pltpu.SemaphoreType.DMA
    results = [((rows, width), BF16), ((chunk, width), BF16)]
    gp, gc = pl.pallas_call(
        functools.partial(kernel, nz),
        out_shape=tuple(pltpu.VMEM(*r) for r in results),
        in_specs=[pl.BlockSpec(memory_space=pl.ANY)] * 4,
        out_specs=[pl.BlockSpec(memory_space=pltpu.VMEM)] * 2,
        scratch_shapes=[
            pltpu.VMEM((rows, width), BF16),
            pltpu.VMEM((pool, width), BF16),
            pltpu.VMEM((1, rows), F32),
            pltpu.VMEM((nblocks, BLOCK, pool), jnp.int32),
            pltpu.VMEM((nblocks, pool, BLOCK), F32),
            pltpu.VMEM((2, pool, BLOCK), jnp.int32),
            pltpu.VMEM((pool, rows), BF16),
            pltpu.VMEM((nz, chunk, rows), BF16),
            pltpu.VMEM((nz, chunk, width), F32),
            pltpu.VMEM((2, rows, width), F32),
            pltpu.VMEM((rows, 128), F32),
            pltpu.VMEM((3, 4, rows), F32),
            pltpu.VMEM((2 * SIDE - 1, 4, rows), F32),
            pltpu.VMEM((2, steps, size, width), BF16),
            pltpu.VMEM((2, steps, size, width), BF16),
            pltpu.VMEM((TURNS, turn, width), BF16),
            pltpu.VMEM((TURNS, turn, width), BF16),
            pltpu.VMEM((TURNS, turn, width), F32),
            pltpu.VMEM((TURNS, turn, width), BF16),
            pltpu.VMEM((TURNS, SIDE - 1, share, width), BF16),
            pltpu.VMEM((TURNS, SIDE, share, width), BF16),
            dma((2 + nz + nblocks,)),
            dma((2 * SIDE - 1, 2)),
            dma((2, steps, 2)),
            dma((TURNS, 2)),
            dma((TURNS, SIDE - 1, 2)),
            dma((TURNS, SIDE - 1, 2)),
            dma((TURNS, SIDE - 1, 2)),
            dma((TURNS, 2)),
        ],
        compiler_params=pltpu.CompilerParams(
            collective_id=0, has_side_effects=True, vmem_limit_bytes=56 * 1024 * 1024
        ),
    )(prompts, cands, positive, cot.reshape(1, rows))
    return pl.pallas_call(
        flush,
        out_shape=tuple(jax.ShapeDtypeStruct(*r) for r in results),
        in_specs=[pl.BlockSpec(memory_space=pl.ANY)] * 2,
        out_specs=[pl.BlockSpec(memory_space=pl.ANY)] * 2,
        scratch_shapes=[dma((2,))],
        compiler_params=pltpu.CompilerParams(vmem_limit_bytes=1024 * 1024),
    )(gp, gc)


def solution(mesh):
    placed = (P("prompt", None), P("pool", None), P("prompt", "pool"), P("prompt"))
    return jax.shard_map(
        functools.partial(local, mesh.shape["prompt"]),
        mesh=mesh,
        in_specs=placed,
        out_specs=(P("prompt", None), P(("pool", "prompt"), None)),
        check_vma=False,
    )
```

```python
import functools
import math

import jax
import jax.numpy as jnp
from jax import lax
from jax.experimental import pallas as pl
from jax.experimental.pallas import tpu as pltpu
from jax.sharding import PartitionSpec as P

NEG_FLOOR = -1e30
LOG2E = 1.4426950408889634
F32 = jnp.float32
BF16 = jnp.bfloat16
SIDE = 4
SHIFTS = (2, 1, 3)
MESH = pl.DeviceIdType.MESH
BLOCK = 256
PARTS = 2
TURNS = 2

ROUTE = [(1, 4)] + [(q, hops) for hops in (3, 2, 1) for q in (0, 1)]
LAG = 2


def kernel(
    nz,
    prompts_hbm,
    cands_hbm,
    positive_hbm,
    cot_hbm,
    gp_ref,
    gc_ref,
    prompts,
    cands,
    cot,
    pos,
    scores,
    pos_t,
    signed,
    weights,
    own,
    raw,
    columns,
    st_send,
    st_recv,
    z_send,
    z_recv,
    p1_send,
    p1_recv,
    p_acc,
    p2_send,
    p2_recv,
    p3_buf,
    load_sem,
    st_sems,
    z_sems,
    p1_sems,
    p2_sems,
    p3_sems,
    p5_sems,
    p6_sems,
):
    rows, width = prompts.shape
    pool = cands.shape[0]
    factor = 2.0 / math.sqrt(width)
    rate = factor * LOG2E
    nblocks = rows // BLOCK
    chunk = pool // nz
    size = chunk // PARTS
    half = rows // 2
    turn = half // TURNS
    share = turn // SIDE

    me = lax.axis_index("pool")
    z = lax.axis_index("prompt")
    core = lax.rem(me, 2)
    x = lax.rem(me // 2, SIDE)
    y = me // (2 * SIDE)
    first = (1 - core) * x + core * y
    second = core * x + (1 - core) * y

    def place(a, b):
        return (((core * a + (1 - core) * b) * SIDE) + (1 - core) * a + core * b) * 2 + core

    sibling = {"pool": me + 1 - 2 * core}
    firsts = [{"pool": place(lax.rem(first + k, SIDE), second)} for k in SHIFTS]
    seconds = [{"pool": place(first, lax.rem(second + k, SIDE))} for k in SHIFTS]
    beside = [{"prompt": lax.rem(z + 1, nz)}, {"prompt": lax.rem(z + nz - 1, nz)}]

    owner = [lax.rem(z + r, nz) for r in range(nz)]

    def spot(r):
        return pl.ds(r * chunk, chunk)

    def source(r):
        return pl.ds(pl.multiple_of(owner[r] * chunk, chunk), chunk)

    load_q = pltpu.make_async_copy(prompts_hbm, prompts, load_sem.at[0])
    load_c = [
        pltpu.make_async_copy(
            cands_hbm.at[source(r), :], cands.at[spot(r), :], load_sem.at[1 + r]
        )
        for r in range(nz)
    ]
    load_p = [
        pltpu.make_async_copy(
            positive_hbm.at[pl.ds(b * BLOCK, BLOCK), :], pos.at[b], load_sem.at[1 + nz + b]
        )
        for b in range(nblocks)
    ]
    load_cot = pltpu.make_async_copy(cot_hbm, cot, load_sem.at[1 + nz + nblocks])
    load_q.start()
    for load in load_c + load_p + [load_cot]:
        load.start()

    barrier = pltpu.get_barrier_semaphore()
    peers = [sibling] + firsts + seconds + beside
    for peer in peers:
        pl.semaphore_signal(barrier, inc=1, device_id=peer, device_id_type=MESH)

    def remote(src, dst, sems, peer):
        return pltpu.make_async_remote_copy(
            src_ref=src,
            dst_ref=dst,
            send_sem=sems.at[0],
            recv_sem=sems.at[1],
            device_id=peer,
            device_id_type=MESH,
        )

    def fold(op, v):
        return op(v.reshape(v.shape[0] // 8, 8, v.shape[1]), axis=0)

    top_all = [None] * nblocks
    top_pos = [None] * nblocks

    def score(b):
        s = lax.dot_general(
            cands[...],
            prompts[pl.ds(b * BLOCK, BLOCK), :],
            (((1,), (1,)), ((), ())),
            preferred_element_type=F32,
        )
        scores[b] = s
        top_all[b] = jnp.max(fold(jnp.max, s), axis=0, keepdims=True)

    def mark(b):
        top = jnp.full((8, BLOCK), NEG_FLOOR, F32)
        for r in range(nz):
            found = pos[b, :, source(r)].T
            pos_t[b % 2, spot(r), :] = found
            kept = jnp.where(found == 1, scores[b, spot(r), :], NEG_FLOOR)
            top = jnp.maximum(top, fold(jnp.max, kept))
        top_pos[b] = jnp.max(top, axis=0, keepdims=True)

    def spread(b):
        cols = pl.ds(b * BLOCK, BLOCK)
        sum_rest = jnp.zeros((8, BLOCK), F32)
        sum_pos = jnp.zeros((8, BLOCK), F32)
        for r in range(nz):
            chosen = pos_t[b % 2, spot(r), :] == 1
            e = jnp.exp2((scores[b, spot(r), :] - jnp.where(chosen, top_pos[b], top_all[b])) * rate)
            rest = jnp.where(chosen, 0.0, e)
            picked = e - rest
            signed[spot(r), cols] = (rest - picked).astype(BF16)
            sum_rest = sum_rest + fold(jnp.sum, rest)
            sum_pos = sum_pos + fold(jnp.sum, picked)
        sum_rest = jnp.sum(sum_rest, axis=0, keepdims=True)
        sum_pos = jnp.sum(sum_pos, axis=0, keepdims=True)
        st_send[0, 0:1, cols] = top_all[b]
        st_send[0, 1:2, cols] = top_pos[b]
        st_send[0, 2:3, cols] = sum_rest + sum_pos * jnp.exp2((top_pos[b] - top_all[b]) * rate)
        st_send[0, 3:4, cols] = sum_pos

    load_q.wait()
    for load in load_c:
        load.wait()
    score(0)
    score(1)
    for b in range(0, nblocks, 2):
        load_p[b].wait()
        load_p[b + 1].wait()
        for c in (b, b + 1):
            if c + 2 < nblocks:
                score(c + 2)
            mark(c)
            spread(c)

    pl.semaphore_wait(barrier, len(peers))

    def merge(parts):
        top = functools.reduce(jnp.maximum, [t[0:2, :] for t in parts])
        total = sum(t[2:4, :] * jnp.exp2((t[0:2, :] - top) * rate) for t in parts)
        return top, total

    def gather(b):
        cols = pl.ds(b * BLOCK, BLOCK)
        e = signed[:, cols]
        zero = jnp.zeros_like(e)
        for kind, part in enumerate((jnp.maximum(e, zero), jnp.minimum(e, zero))):
            raw[kind, cols, :] = lax.dot_general(
                part, cands[...], (((0,), (0,)), ((), ())), preferred_element_type=F32
            )

    swap = remote(st_send.at[0], st_recv.at[0], st_sems.at[0], sibling)
    swap.start()
    sent = [swap]
    swap.wait_recv()
    top, total = merge([st_send.at[0], st_recv.at[0]])
    for stage, group in ((1, firsts), (2, seconds)):
        st_send[stage, 0:2, :] = top
        st_send[stage, 2:4, :] = total
        at = 1 + (stage - 1) * (SIDE - 1)
        copies = [
            remote(st_send.at[stage], st_recv.at[at + k], st_sems.at[at + k], peer)
            for k, peer in enumerate(group)
        ]
        for copy in copies:
            copy.start()
        for b in range((stage - 1) * nblocks // 2, stage * nblocks // 2):
            gather(b)
        for copy in copies:
            copy.wait_recv()
        sent += copies
        top, total = merge([st_send.at[stage]] + [st_recv.at[at + k] for k in range(SIDE - 1)])

    local_top = st_send[0, 0:2, :]
    load_cot.wait()
    gain = cot[...] * factor
    down = gain * jnp.exp2((local_top - top) * rate) / total
    cross = gain * jnp.exp2((local_top[1:2, :] - top[0:1, :]) * rate) / total[0:1, :]
    scale_rest = down[0:1, :]
    scale_pos = down[1:2, :] - cross

    def project(r):
        e = signed[spot(r), :].astype(F32)
        weights[r] = (e * jnp.where(e < 0.0, scale_pos, scale_rest)).astype(BF16)
        own[r] = jnp.dot(weights[r], prompts[...], preferred_element_type=F32)

    def z_piece(way, i):
        q, hops = ROUTE[i]
        return (q if way == 0 else PARTS - 1 - q), (hops if way == 0 else nz - hops)

    def z_copy(way, i):
        return remote(z_send.at[way, i], z_recv.at[way, i], z_sems.at[way, i], beside[way])

    def z_push(i):
        for way in (0, 1):
            q, r = z_piece(way, i)
            value = own[r, q * size : (q + 1) * size, :]
            if i >= LAG:
                z_copy(way, i - LAG).wait_recv()
                value = value + z_recv[way, i - LAG].astype(F32)
            z_send[way, i] = value.astype(BF16)
            z_copy(way, i).start()

    project(nz // 2)
    z_push(0)
    project(3)
    project(nz - 3)
    z_push(1)

    lanes = jnp.concatenate(
        [scale_rest, scale_pos, jnp.zeros((6, rows), F32)], axis=0
    )
    columns[:, 0:8] = lanes.T
    mine = core * half

    def scaled(start):
        at = pl.ds(pl.multiple_of(start, turn), turn)
        return raw[0, at, :] * columns[at, 0:1] + raw[1, at, :] * columns[at, 1:2]

    p1 = []
    for u in range(TURNS):
        p1_send[u] = scaled(half - mine + u * turn).astype(BF16)
        p1.append(remote(p1_send.at[u], p1_recv.at[u], p1_sems.at[u], sibling))
        p1[u].start()
    for u in range(TURNS):
        p_acc[u] = scaled(mine + u * turn)

    def my_share(a):
        return pl.ds(pl.multiple_of(a * share, share), share)

    def p2_copy(u, k):
        return remote(
            p2_send.at[u, my_share(lax.rem(first + SHIFTS[k], SIDE)), :],
            p2_recv.at[u, k],
            p2_sems.at[u, k],
            firsts[k],
        )

    def p3_copy(u, k):
        return remote(p3_buf.at[u, second], p3_buf.at[u, second], p3_sems.at[u, k], seconds[k])

    def p5_copy(u, k):
        at = pl.ds(pl.multiple_of(mine + u * turn + first * share, share), share)
        return remote(gp_ref.at[at, :], gp_ref.at[at, :], p5_sems.at[u, k], firsts[k])

    def p6_copy(u):
        at = pl.ds(pl.multiple_of(mine + u * turn, turn), turn)
        return remote(gp_ref.at[at, :], gp_ref.at[at, :], p6_sems.at[u], sibling)

    def p2_go(u):
        p1[u].wait_recv()
        value = p_acc[u] + p1_recv[u].astype(F32)
        p_acc[u] = value
        p2_send[u] = value.astype(BF16)
        for k in range(SIDE - 1):
            p2_copy(u, k).start()

    def p3_go(u):
        for k in range(SIDE - 1):
            p2_copy(u, k).wait_recv()
        value = p_acc[u, my_share(first), :] + sum(
            p2_recv[u, k].astype(F32) for k in range(SIDE - 1)
        )
        p3_buf[u, second] = value.astype(BF16)
        for k in range(SIDE - 1):
            p3_copy(u, k).start()

    def p5_go(u):
        for k in range(SIDE - 1):
            p3_copy(u, k).wait_recv()
        value = sum(p3_buf[u, b].astype(F32) for b in range(SIDE))
        at = pl.ds(pl.multiple_of(mine + u * turn + first * share, share), share)
        gp_ref[at, :] = value.astype(BF16)
        for k in range(SIDE - 1):
            p5_copy(u, k).start()

    def p6_go(u):
        for k in range(SIDE - 1):
            p5_copy(u, k).wait_recv()
        p6_copy(u).start()

    project(2)
    p2_go(0)
    p2_go(1)
    project(nz - 2)
    z_push(2)
    project(1)
    p3_go(0)
    z_push(3)
    p3_go(1)
    project(nz - 1)
    z_push(4)
    project(0)
    p5_go(0)
    z_push(5)
    p5_go(1)
    z_push(6)
    p6_go(0)
    p6_go(1)

    last = len(ROUTE) - LAG
    for i in range(last, len(ROUTE)):
        for way in (0, 1):
            z_copy(way, i).wait_recv()
    for q in range(PARTS):
        value = own[0, q * size : (q + 1) * size, :]
        for i in range(last, len(ROUTE)):
            for way in (0, 1):
                if z_piece(way, i)[0] == q:
                    value = value + z_recv[way, i].astype(F32)
        gc_ref[q * size : (q + 1) * size, :] = value.astype(BF16)
    for i in range(len(ROUTE)):
        for way in (0, 1):
            z_copy(way, i).wait_send()
    for copy in sent + p1:
        copy.wait_send()
    for u in range(TURNS):
        for k in range(SIDE - 1):
            p2_copy(u, k).wait_send()
            p3_copy(u, k).wait_send()
            p5_copy(u, k).wait_send()
        p6_copy(u).wait()


def flush(gp, gc, gp_out, gc_out, sems):
    copies = [
        pltpu.make_async_copy(gp, gp_out, sems.at[0]),
        pltpu.make_async_copy(gc, gc_out, sems.at[1]),
    ]
    for copy in copies:
        copy.start()
    for copy in copies:
        copy.wait()


def local(nz, prompts, cands, positive, cot):
    rows, width = prompts.shape
    pool = cands.shape[0]
    nblocks = rows // BLOCK
    chunk = pool // nz
    size = chunk // PARTS
    turn = rows // 2 // TURNS
    share = turn // SIDE
    steps = len(ROUTE)
    dma = pltpu.SemaphoreType.DMA
    results = [((rows, width), BF16), ((chunk, width), BF16)]
    gp, gc = pl.pallas_call(
        functools.partial(kernel, nz),
        out_shape=tuple(pltpu.VMEM(*r) for r in results),
        in_specs=[pl.BlockSpec(memory_space=pl.ANY)] * 4,
        out_specs=[pl.BlockSpec(memory_space=pltpu.VMEM)] * 2,
        scratch_shapes=[
            pltpu.VMEM((rows, width), BF16),
            pltpu.VMEM((pool, width), BF16),
            pltpu.VMEM((1, rows), F32),
            pltpu.VMEM((nblocks, BLOCK, pool), jnp.int32),
            pltpu.VMEM((nblocks, pool, BLOCK), F32),
            pltpu.VMEM((2, pool, BLOCK), jnp.int32),
            pltpu.VMEM((pool, rows), BF16),
            pltpu.VMEM((nz, chunk, rows), BF16),
            pltpu.VMEM((nz, chunk, width), F32),
            pltpu.VMEM((2, rows, width), F32),
            pltpu.VMEM((rows, 128), F32),
            pltpu.VMEM((3, 4, rows), F32),
            pltpu.VMEM((2 * SIDE - 1, 4, rows), F32),
            pltpu.VMEM((2, steps, size, width), BF16),
            pltpu.VMEM((2, steps, size, width), BF16),
            pltpu.VMEM((TURNS, turn, width), BF16),
            pltpu.VMEM((TURNS, turn, width), BF16),
            pltpu.VMEM((TURNS, turn, width), F32),
            pltpu.VMEM((TURNS, turn, width), BF16),
            pltpu.VMEM((TURNS, SIDE - 1, share, width), BF16),
            pltpu.VMEM((TURNS, SIDE, share, width), BF16),
            dma((2 + nz + nblocks,)),
            dma((2 * SIDE - 1, 2)),
            dma((2, steps, 2)),
            dma((TURNS, 2)),
            dma((TURNS, SIDE - 1, 2)),
            dma((TURNS, SIDE - 1, 2)),
            dma((TURNS, SIDE - 1, 2)),
            dma((TURNS, 2)),
        ],
        compiler_params=pltpu.CompilerParams(
            collective_id=0, has_side_effects=True, vmem_limit_bytes=56 * 1024 * 1024
        ),
    )(prompts, cands, positive, cot.reshape(1, rows))
    return pl.pallas_call(
        flush,
        out_shape=tuple(jax.ShapeDtypeStruct(*r) for r in results),
        in_specs=[pl.BlockSpec(memory_space=pl.ANY)] * 2,
        out_specs=[pl.BlockSpec(memory_space=pl.ANY)] * 2,
        scratch_shapes=[dma((2,))],
        compiler_params=pltpu.CompilerParams(vmem_limit_bytes=1024 * 1024),
    )(gp, gc)


def solution(mesh):
    placed = (P("prompt", None), P("pool", None), P("prompt", "pool"), P("prompt"))
    return jax.shard_map(
        functools.partial(local, mesh.shape["prompt"]),
        mesh=mesh,
        in_specs=placed,
        out_specs=(P("prompt", None), P(("pool", "prompt"), None)),
        check_vma=False,
    )
```
